32 devices in a mesh: blk: 8 (over y, x, core), feat: 4 (over z).
Axes of the slice: x: 2, y: 2, z: 4, core: 2. Of those that a mesh axis runs over, the one named last changes fastest.
Arguments:
- features: bfloat16 [256, 16384], P('feat', 'blk'), may hold values from -6 to 6
- adj_tiles: bfloat16 [8, 4, 8, 48, 128, 128], P('blk', 'feat'), may hold values from -0.0546875 to 0.0546875
- tile_rows: int32 [8, 4, 8, 48], P('blk', 'feat'), may hold values from 0 to 15
- tile_cols: int32 [8, 4, 8, 48], P('blk', 'feat'), may hold values from 0 to 15
- counts: int32 [8, 4, 8], P('blk', 'feat'), may hold values from 1 to 48, as said below
- weight: bfloat16 [256, 256], replicated, may hold values from -0.375 to 0.375
- cotangent: bfloat16 [256, 16384], P(None, ('blk', 'feat')), may hold values from -6 to 6
Outputs:
- activated: bfloat16 [256, 16384], P(None, ('blk', 'feat'))
- weight_grad: float32 [256, 256], P('feat')
The draws below stay inside these ranges and needn't reach their ends.
Inputs may be any that keep to these rules, and one draw needn't show every extreme that they name: Only the first counts slots of a partition, group and source partition are live; the slots a partition takes from its own nodes are all live in every group.
All inputs are finite; a program needn't handle non-finite values.
Results may differ from the reference program's by a relative error of at most 0.02.
Values may be sent and summed in bfloat16 or wider, within the bound.
No kernel may reach another device: no remote copies, remote signals or barrier semaphores. Data moves between devices by JAX's collectives and lax.ppermute only.
A program may use at most 320 MiB of HBM per device.

```python
import math
import jax
import jax.numpy as jnp
from jax import lax

F = 256
TILE = 128
ROWS = 2048
CAPF = 48
NODES = 16384
N_BLK = 8
N_FEAT = 4


def draw_counts(key, part):
    first_key, second_key = jax.random.split(jax.random.fold_in(key, 11))
    level_pick = jax.random.randint(first_key, (N_BLK, 1, 1), 0, 4)
    levels = jnp.array([1, 2, 4, 8], dtype=jnp.int32)
    level_val = jnp.take(levels, level_pick)
    base_val = jax.random.randint(second_key, (N_BLK, N_FEAT, N_BLK), 1, CAPF + 1)
    counts_val = jnp.clip(base_val * level_val // 8, 1, CAPF)
    own_part = jnp.arange(N_BLK)[:, None, None] == jnp.arange(N_BLK)[None, None, :]
    return jnp.where(own_part, CAPF, counts_val).astype(jnp.int32)


def plant(values, own_key, low, top_value):
    dims = values.shape
    place = [jax.random.randint(jax.random.fold_in(own_key, axis), (), 0, dims[axis]) for axis in range(len(dims))]
    values = values.at[tuple(place)].set(low)
    longest = dims.index(max(dims))
    place[longest] = (place[longest] + 1) % dims[longest]
    return values.at[tuple(place)].set(top_value)


def shard_levels(key, dims, cuts, least, largest):
    factor_of, own = 1.0, jax.random.fold_in(key, 6)
    for dim, shards_of in cuts:
        steps = jnp.exp(jax.random.uniform(jax.random.fold_in(own, dim), (shards_of,), jnp.float32, least / len(cuts), largest / len(cuts)))
        factor_of = factor_of * jnp.repeat(steps, dims[dim] // shards_of).reshape([-1 if axis == dim else 1 for axis in range(len(dims))])
    return factor_of


def scatter_about(own_key, shape, width, limit, pieces=(), kind=jnp.bfloat16):
    factor_of = shard_levels(own_key, shape, pieces, -0.22, 0.18) if pieces else 1.0
    result = jax.random.normal(own_key, shape, jnp.float32) * width * factor_of
    return jnp.minimum(jnp.maximum(result, -limit), limit).astype(kind)


def setup_inputs(seed: int = 0) -> dict:
    arg_keys = jax.random.split(jax.random.key(seed), 8)
    features = scatter_about(arg_keys[0], (F, NODES), 1.0, 6.0, ((0, 4), (1, 8)))
    adj_tiles = scatter_about(arg_keys[1], (N_BLK, N_FEAT, N_BLK, CAPF, TILE, TILE), (TILE * N_BLK * N_FEAT * CAPF // (ROWS // TILE)) ** -0.5, 0.0546875, ((0, 8), (1, 4)))
    tile_rows = plant(jax.random.randint(arg_keys[2], (N_BLK, N_FEAT, N_BLK, CAPF), 0, ROWS // TILE), jax.random.fold_in(arg_keys[2], 1), 0, (ROWS // TILE) - 1).astype(jnp.int32)
    tile_cols = plant(jax.random.randint(arg_keys[3], (N_BLK, N_FEAT, N_BLK, CAPF), 0, ROWS // TILE), jax.random.fold_in(arg_keys[3], 1), 0, (ROWS // TILE) - 1).astype(jnp.int32)
    counts = draw_counts(jax.random.fold_in(arg_keys[7], 71), 0)
    weight = scatter_about(arg_keys[5], (F, F), F ** -0.5, 0.375)
    cotangent = scatter_about(arg_keys[6], (F, NODES), 1.0, 6.0, ((1, 32),))
    return {"features": features, "adj_tiles": adj_tiles, "tile_rows": tile_rows, "tile_cols": tile_cols, "counts": counts, "weight": weight, "cotangent": cotangent}


def partition_terms(part_index, features, adj_tiles, tile_rows, tile_cols, counts):
    row_tiles = ROWS // TILE
    col_panels = features.reshape(F, N_BLK * row_tiles, TILE)
    sources = jnp.arange(N_BLK, dtype=jnp.int32)
    slot_index = jnp.arange(CAPF, dtype=jnp.int32)
    tile_range = jnp.arange(row_tiles, dtype=jnp.int32)

    def add_group(group_idx, running):
        block = adj_tiles[part_index, group_idx].reshape(N_BLK * CAPF, TILE, TILE)
        rows_here = tile_rows[part_index, group_idx].reshape(-1).astype(jnp.int32)
        cols_here = (sources[:, None] * row_tiles + tile_cols[part_index, group_idx].astype(jnp.int32)).reshape(-1)
        live_mask = (slot_index[None, :] < counts[part_index, group_idx][:, None]).reshape(-1)
        gathered = jnp.take(col_panels, cols_here, axis=1)
        products = jnp.einsum('kij,fkj->fki', block.astype(jnp.float32), gathered.astype(jnp.float32), precision=lax.Precision.HIGHEST)
        placing = ((rows_here[:, None] == tile_range[None, :]) & live_mask[:, None]).astype(jnp.float32)
        summed = jnp.einsum('fki,kr->fri', products, placing, precision=lax.Precision.HIGHEST)
        return running + summed.reshape(F, ROWS)
    return lax.fori_loop(0, N_FEAT, add_group, jnp.zeros((F, ROWS), jnp.float32))

def reference(features, adj_tiles, tile_rows, tile_cols, counts, weight, cotangent):
    per_part = lax.map(lambda part_index: partition_terms(part_index, features, adj_tiles, tile_rows, tile_cols, counts), jnp.arange(N_BLK, dtype=jnp.int32))
    aggregated = jnp.transpose(per_part, (1, 0, 2)).reshape(F, NODES).astype(jnp.bfloat16)
    preact = jnp.dot(weight, aggregated, preferred_element_type=jnp.float32)
    activated = (preact * jax.nn.sigmoid(preact)).astype(jnp.bfloat16)
    sigmoid_z = jax.nn.sigmoid(preact)
    slope = (cotangent.astype(jnp.float32) * sigmoid_z * (1.0 + preact * (1.0 - sigmoid_z))).astype(jnp.bfloat16)
    weight_grad = lax.dot_general(slope, aggregated, (((1,), (1,)), ((), ())), preferred_element_type=jnp.float32)
    weight_grad = weight_grad * (1.0 / math.sqrt(NODES))
    return (activated, weight_grad)
```

```python
import functools
import math

import jax
import jax.numpy as jnp
from jax import lax
from jax.experimental import pallas as pl
from jax.experimental.pallas import tpu as pltpu
from jax.sharding import PartitionSpec as P

CHUNK = 8
UNROLL = 4


def hop(value, axis, bit):
    size = lax.axis_size(axis)
    return lax.ppermute(value, axis, [(i, i ^ bit) for i in range(size)])


def aggregate_kernel(offsets, groups, first, last, *refs):
    n_src = len(offsets)
    rows_ref, cols_ref, counts_ref, tiles_ref = refs[:4]
    unit_refs = refs[4 : 4 + n_src * groups]
    rest = refs[4 + n_src * groups :]
    if first:
        out_refs, scratch = rest[:1], rest[1:]
    elif last:
        acc_in, out_refs, scratch = rest[0], rest[1:3], rest[3:]
    else:
        acc_in, out_refs, scratch = rest[0], rest[1:2], rest[2:]
    feat, tiles, acc, unit_sems, tile_sems, acc_sem = scratch
    blk = lax.axis_index("blk")
    z = lax.axis_index("feat")
    slots = tiles_ref.shape[1]
    size = tiles_ref.shape[2]
    width = unit_refs[0].shape[0]
    nodes = unit_refs[0].shape[1]
    row_tiles = nodes // size
    chunks = slots // CHUNK

    def unit_copy(i, k):
        start = pl.multiple_of(lax.bitwise_xor(z, k) * width, width)
        return pltpu.make_async_copy(
            unit_refs[i * groups + k],
            feat.at[i, pl.ds(start, width), :],
            unit_sems.at[i, k],
        )

    def tile_copy(i, source, chunk):
        at = pl.ds(chunk * CHUNK, CHUNK)
        return pltpu.make_async_copy(tiles_ref.at[source, at], tiles.at[i, at], tile_sems.at[i, chunk])

    sources = [lax.bitwise_xor(blk, jnp.int32(off)) for off in offsets]
    live = [counts_ref[source] for source in sources]
    if not first:
        acc_copy = pltpu.make_async_copy(acc_in, acc.at[pl.ds(0, nodes)], acc_sem)
        acc_copy.start()
    for i in range(n_src):
        for k in range(groups):
            unit_copy(i, k).start()
        for chunk in range(chunks):

            @pl.when(chunk * CHUNK < live[i])
            def _():
                tile_copy(i, sources[i], chunk).start()

    if first:
        acc[pl.ds(0, nodes), :] = jnp.zeros((nodes, acc.shape[1]), jnp.float32)
    else:
        acc_copy.wait()
    for i in range(n_src):
        for k in range(groups):
            unit_copy(i, k).wait()

        def do_chunk(chunk, _):
            tile_copy(i, sources[i], chunk).wait()

            def do_some(part, _):
                base = chunk * CHUNK + part * UNROLL
                for u in range(UNROLL):
                    slot = base + u
                    row = jnp.where(slot < live[i], rows_ref[sources[i], slot], row_tiles)
                    col = cols_ref[sources[i], slot]
                    at = pl.ds(pl.multiple_of(row * size, size), size)
                    term = lax.dot_general(
                        tiles[i, slot],
                        feat[i, :, pl.ds(pl.multiple_of(col * size, size), size)],
                        (((1,), (1,)), ((), ())),
                        preferred_element_type=jnp.float32,
                    )
                    acc[at, :] += term
                return 0

            parts = jnp.minimum((live[i] - chunk * CHUNK + UNROLL - 1) // UNROLL, CHUNK // UNROLL)
            return lax.fori_loop(0, parts, do_some, 0)

        lax.fori_loop(0, (live[i] + CHUNK - 1) // CHUNK, do_chunk, 0)
    if last:
        send_ref, keep_ref = out_refs
        share = nodes // groups
        mine = lax.rem(z, 2)
        for d in range(groups // 2):
            keep_at = pl.multiple_of((2 * d + mine) * share, share)
            send_at = pl.multiple_of((2 * d + 1 - mine) * share, share)
            send_ref[d] = acc[pl.ds(send_at, share), :].astype(jnp.bfloat16)
            keep_ref[d] = acc[pl.ds(keep_at, share), :]
    else:
        out_copy = pltpu.make_async_copy(acc.at[pl.ds(0, nodes)], out_refs[0], acc_sem)
        out_copy.start()
        out_copy.wait()


def aggregate(offsets, groups, rows, cols, counts, tiles, units, acc, last):
    n_src = len(offsets)
    slots, size = tiles.shape[1], tiles.shape[2]
    width, nodes = units[0].shape
    feat_width = width * groups
    first = acc is None
    any_spec = pl.BlockSpec(memory_space=pl.ANY)
    smem = pl.BlockSpec(memory_space=pltpu.SMEM)
    vmem = pl.BlockSpec(memory_space=pltpu.VMEM)
    share = nodes // groups
    if last:
        out_shape = (
            jax.ShapeDtypeStruct((groups // 2, share, feat_width), jnp.bfloat16),
            jax.ShapeDtypeStruct((groups // 2, share, feat_width), jnp.float32),
        )
        out_specs = (vmem, vmem)
    else:
        out_shape = jax.ShapeDtypeStruct((nodes, feat_width), jnp.float32)
        out_specs = any_spec
    extra = [] if first else [acc]
    return pl.pallas_call(
        functools.partial(aggregate_kernel, offsets, groups, first, last),
        out_shape=out_shape,
        in_specs=[smem] * 3 + [any_spec] * (1 + len(units) + len(extra)),
        out_specs=out_specs,
        scratch_shapes=[
            pltpu.VMEM((n_src, feat_width, nodes), jnp.bfloat16),
            pltpu.VMEM((n_src, slots, size, size), jnp.bfloat16),
            pltpu.VMEM((nodes + size, feat_width), jnp.float32),
            pltpu.SemaphoreType.DMA((n_src, groups)),
            pltpu.SemaphoreType.DMA((n_src, slots // CHUNK)),
            pltpu.SemaphoreType.DMA,
        ],
        compiler_params=pltpu.CompilerParams(vmem_limit_bytes=40 * 1024 * 1024),
    )(rows, cols, counts, tiles, *units, *extra)


def low_bit(m):
    return m & -m


def high_bit(m):
    return 1 << (m.bit_length() - 1)


def shards(features, adj_tiles, tile_rows, tile_cols, counts, weight, cotangent):
    blocks = lax.axis_size("blk")
    groups = lax.axis_size("feat")
    width, nodes = features.shape
    feat_width = width * groups
    tile_size = adj_tiles.shape[-1]
    slot_cap = adj_tiles.shape[3]
    tiles = adj_tiles.reshape(blocks, slot_cap, tile_size, tile_size)
    rows = tile_rows.reshape(blocks, slot_cap)
    cols = tile_cols.reshape(blocks, slot_cap)
    live = counts.reshape(blocks)
    z = lax.axis_index("feat")
    chips = blocks // 2

    held = {(0, 0): features}
    for k in range(1, groups):
        bit = low_bit(k)
        held[k, 0] = hop(held[k ^ bit, 0], "feat", bit)
    for k in range(groups):
        for m in range(1, chips):
            bit = low_bit(m) if k % 2 == 0 else high_bit(m)
            held[k, m] = hop(held[k, m ^ bit], "blk", 2 * bit)
    other = {key: hop(value, "blk", 1) for key, value in held.items()}

    weights_of = [bin(m).count("1") for m in range(chips)]
    acc = None
    stages = sorted(set(weights_of))
    for stage in stages:
        offsets, units = [], []
        for m in range(chips):
            if weights_of[m] == stage:
                for side, table in ((0, held), (1, other)):
                    offsets.append(2 * m + side)
                    units += [table[k, m] for k in range(groups)]
        acc = aggregate(tuple(offsets), groups, rows, cols, live, tiles, units, acc, stage == stages[-1])
    send, keep = acc
    total = keep + hop(send, "feat", 1).astype(jnp.float32)
    bit = 2
    while bit < groups:
        mine = lax.rem(z // bit, 2)
        pairs = total.reshape(total.shape[0] // 2, 2, *total.shape[1:])
        send = lax.dynamic_index_in_dim(pairs, 1 - mine, 1, False).astype(jnp.bfloat16)
        keep = lax.dynamic_index_in_dim(pairs, mine, 1, False)
        total = keep + hop(send, "feat", bit).astype(jnp.float32)
        bit *= 2
    aggregated = total[0].astype(jnp.bfloat16)

    preact = lax.dot_general(
        weight, aggregated, (((1,), (1,)), ((), ())), preferred_element_type=jnp.float32
    )
    sigmoid_z = jax.nn.sigmoid(preact)
    activated = (preact * sigmoid_z).astype(jnp.bfloat16)
    slope = (cotangent.astype(jnp.float32) * sigmoid_z * (1.0 + preact * (1.0 - sigmoid_z))).astype(
        jnp.bfloat16
    )
    local_grad = jnp.dot(slope, aggregated, preferred_element_type=jnp.float32)
    terms = lax.all_to_all(
        local_grad.astype(jnp.bfloat16).reshape(groups, feat_width // groups, feat_width), "feat", 0, 0
    )
    grad = jnp.sum(terms.astype(jnp.float32), axis=0)
    sent = grad.astype(jnp.bfloat16)
    grad = sent.astype(jnp.float32) + hop(sent, "blk", 1).astype(jnp.float32)
    sent = grad.astype(jnp.bfloat16)
    parts = [(hop(sent, "blk", 2 * m) if m else sent).astype(jnp.float32) for m in range(chips)]
    while len(parts) > 1:
        parts = [parts[i] + parts[i + 1] for i in range(0, len(parts), 2)]
    return activated, parts[0] * (1.0 / math.sqrt(blocks * nodes))


def solution(mesh):
    in_specs = (
        P("feat", "blk"),
        P("blk", "feat", None, None, None, None),
        P("blk", "feat", None, None),
        P("blk", "feat", None, None),
        P("blk", "feat", None),
        P(),
        P(None, ("blk", "feat")),
    )
    out_specs = (P(None, ("blk", "feat")), P("feat", None))
    return jax.shard_map(shards, mesh=mesh, in_specs=in_specs, out_specs=out_specs, check_vma=False)
```

```python
import functools
import math

import jax
import jax.numpy as jnp
from jax import lax
from jax.experimental import pallas as pl
from jax.experimental.pallas import tpu as pltpu
from jax.sharding import PartitionSpec as P

CHUNK = 8
EARLY = 10**10
WIDE = 16


def hop(value, axis, bit):
    size = lax.axis_size(axis)
    return lax.ppermute(value, axis, [(i, i ^ bit) for i in range(size)])


def in_hbm(*values):
    return [pltpu.with_memory_space_constraint(value, pltpu.HBM) for value in values]


def in_vmem(*values):
    return [pltpu.with_memory_space_constraint(value, pltpu.VMEM) for value in values]


def pair_kernel(own_ref, sibling_ref, *refs):
    core = lax.rem(lax.axis_index("blk"), 2)
    refs[-1][core] = own_ref[...]
    refs[-1][1 - core] = sibling_ref[...]


def pick_kernel(even_ref, odd_ref, *refs):
    core = lax.rem(lax.axis_index("blk"), 2)

    @pl.when(core == 0)
    def _():
        refs[-1][...] = even_ref[...]

    @pl.when(core == 1)
    def _():
        refs[-1][...] = odd_ref[...]


def pick_part_kernel(pair_ref, *refs):
    refs[-1][...] = pair_ref[lax.rem(lax.axis_index("blk"), 2)]


def copying(kernel, shape, values, earlier, flops=0):
    vmem = pl.BlockSpec(memory_space=pltpu.VMEM)
    return pl.pallas_call(
        kernel,
        out_shape=pltpu.VMEM(shape, values[0].dtype),
        in_specs=[vmem] * len(values) + [pl.BlockSpec(memory_space=pl.ANY)] * len(earlier),
        out_specs=vmem,
        compiler_params=pltpu.CompilerParams(vmem_limit_bytes=1024 * 1024),
        cost_estimate=pl.CostEstimate(
            flops=flops, bytes_accessed=4 * math.prod(shape), transcendentals=0
        ),
    )(*in_vmem(*values), *earlier)


def same_kernel(value_ref, *refs):
    refs[-1][...] = value_ref[...]


def after(value, *earlier, flops=0):
    return copying(same_kernel, value.shape, [value], earlier, flops)


def pair_of(own, sibling, *earlier):
    return copying(pair_kernel, (2, *own.shape), [own, sibling], earlier)


def pick(even, odd, *earlier):
    return copying(pick_kernel, even.shape, [even, odd], earlier)


def pick_part(pair, *earlier):
    return copying(pick_part_kernel, pair.shape[1:], [pair], earlier)


def aggregate_kernel(sources, n_units, n_earlier, halves, first, *refs):
    *list_hbm, tiles_ref = refs[:4]
    unit_refs = refs[4 : 4 + n_units]
    rest = list(refs[4 + n_units + n_earlier :])
    acc_in = None if first else rest.pop(0)
    n_out = 4 if halves else 1
    out_refs = rest[:n_out]
    rows_ref, cols_ref, counts_ref, feat, tiles, acc, unit_sems, tile_sems, list_sems, acc_sem = rest[n_out:]
    blk = lax.axis_index("blk")
    z = lax.axis_index("feat")
    n_src = len(sources)
    groups = len(sources[0][1])
    slots = tiles_ref.shape[3]
    size = tiles_ref.shape[4]
    width, nodes = unit_refs[0].shape[-2:]
    row_tiles = nodes // size
    chunks = slots // CHUNK
    odd = lax.rem(blk, 2) == 1

    def unit_copy(i, k, side=0):
        unit, part = sources[i][1][k][side]
        ref = unit_refs[unit] if part is None else unit_refs[unit].at[part]
        start = pl.multiple_of(lax.bitwise_xor(z, jnp.int32(k)) * width, width)
        return pltpu.make_async_copy(ref, feat.at[i, pl.ds(start, width), :], unit_sems.at[i, k])

    def start_unit_copy(i, k):
        even, on_odd = sources[i][1][k]
        if even == on_odd:
            unit_copy(i, k).start()
            return
        pl.when(jnp.logical_not(odd))(lambda: unit_copy(i, k, 0).start())
        pl.when(odd)(lambda: unit_copy(i, k, 1).start())

    def tile_copy(i, chunk):
        at = pl.ds(chunk * CHUNK, CHUNK)
        return pltpu.make_async_copy(
            tiles_ref.at[0, 0, parts[i], at], tiles.at[i, at], tile_sems.at[i, chunk]
        )

    list_copies = [
        pltpu.make_async_copy(source, target, list_sems.at[i])
        for i, (source, target) in enumerate(zip(list_hbm, (rows_ref, cols_ref, counts_ref)))
    ]
    for copy in list_copies:
        copy.start()
    if not first:
        acc_copy = pltpu.make_async_copy(acc_in, acc.at[pl.ds(0, nodes)], acc_sem)
        acc_copy.start()
    for i in range(n_src):
        for k in range(groups):
            start_unit_copy(i, k)
    for copy in list_copies:
        copy.wait()
    parts = [lax.bitwise_xor(blk, jnp.int32(off)) for off, _ in sources]
    live = [counts_ref[0, 0, part] for part in parts]
    for i in range(n_src):
        for chunk in range(chunks):

            @pl.when(chunk * CHUNK < live[i])
            def _():
                tile_copy(i, chunk).start()

    if first:
        acc[pl.ds(0, nodes), :] = jnp.zeros((nodes, acc.shape[1]), jnp.float32)
    else:
        acc_copy.wait()
    for i in range(n_src):
        for k in range(groups):
            unit_copy(i, k).wait()
        for chunk in range(chunks):

            @pl.when(chunk * CHUNK < live[i])
            def _():
                tile_copy(i, chunk).wait()

        def add_tiles(base, count):
            for u in range(count):
                slot = base + u
                row = jnp.where(slot < live[i], rows_ref[0, 0, parts[i], slot], row_tiles)
                col = cols_ref[0, 0, parts[i], slot]
                term = lax.dot_general(
                    tiles[i, slot],
                    feat[i, :, pl.ds(pl.multiple_of(col * size, size), size)],
                    (((1,), (1,)), ((), ())),
                    preferred_element_type=jnp.float32,
                )
                acc[pl.ds(pl.multiple_of(row * size, size), size), :] += term
            return 0

        wide = live[i] // WIDE
        left = (live[i] - wide * WIDE + CHUNK - 1) // CHUNK
        lax.fori_loop(0, wide, lambda p, _: add_tiles(p * WIDE, WIDE), 0)
        lax.fori_loop(0, left, lambda p, _: add_tiles(wide * WIDE + p * CHUNK, CHUNK), 0)
    if not halves:
        out_copy = pltpu.make_async_copy(acc.at[pl.ds(0, nodes)], out_refs[0], acc_sem)
        out_copy.start()
        out_copy.wait()
        return
    share = nodes // groups
    half = share // 2
    for part, bit in ((0, 1), (1, 2)):
        send_ref, keep_ref = out_refs[2 * part : 2 * part + 2]
        for j, step in enumerate((0, 3 ^ bit)):
            mine = lax.bitwise_xor(z, jnp.int32(step)) * share + part * half
            theirs = lax.bitwise_xor(z, jnp.int32(step ^ bit)) * share + part * half
            keep_ref[j] = acc[pl.ds(pl.multiple_of(mine, half), half), :]
            send_ref[j] = acc[pl.ds(pl.multiple_of(theirs, half), half), :].astype(jnp.bfloat16)


def aggregate(sources, lists, units, acc, halves, earlier=()):
    rows, cols, counts, tiles = lists
    n_src = len(sources)
    groups = len(sources[0][1])
    slots, size = tiles.shape[3], tiles.shape[4]
    width, nodes = units[0].shape[-2:]
    feat_width = width * groups
    any_spec = pl.BlockSpec(memory_space=pl.ANY)
    vmem = pl.BlockSpec(memory_space=pltpu.VMEM)
    if halves:
        dims = (2, nodes // groups // 2, feat_width)
        out_shape = [jax.ShapeDtypeStruct(dims, jnp.bfloat16), jax.ShapeDtypeStruct(dims, jnp.float32)] * 2
        out_spec = vmem
    else:
        out_shape = [jax.ShapeDtypeStruct((nodes, feat_width), jnp.float32)]
        out_spec = any_spec
    extra = [] if acc is None else [acc]
    return pl.pallas_call(
        functools.partial(aggregate_kernel, sources, len(units), len(earlier), halves, acc is None),
        out_shape=tuple(out_shape),
        in_specs=[any_spec] * (4 + len(units) + len(earlier) + len(extra)),
        out_specs=(out_spec,) * len(out_shape),
        scratch_shapes=[
            pltpu.SMEM(rows.shape, jnp.int32),
            pltpu.SMEM(cols.shape, jnp.int32),
            pltpu.SMEM(counts.shape, jnp.int32),
            pltpu.VMEM((n_src, feat_width, nodes), jnp.bfloat16),
            pltpu.VMEM((n_src, slots, size, size), jnp.bfloat16),
            pltpu.VMEM((nodes + size, feat_width), jnp.float32),
            pltpu.SemaphoreType.DMA((n_src, groups)),
            pltpu.SemaphoreType.DMA((n_src, slots // CHUNK)),
            pltpu.SemaphoreType.DMA((3,)),
            pltpu.SemaphoreType.DMA,
        ],
        compiler_params=pltpu.CompilerParams(vmem_limit_bytes=(6 + 3 * n_src) * 1024 * 1024),
        cost_estimate=pl.CostEstimate(
            flops=2 * n_src * slots * size * size * feat_width * 4,
            bytes_accessed=n_src * (slots * size * size + feat_width * nodes) * 2,
            transcendentals=0,
        ),
    )(*in_hbm(rows, cols, counts, tiles), *units, *earlier, *extra)


def low_bit(m):
    return m & -m


def plain(first, groups):
    return tuple(((first + k, None),) * 2 for k in range(groups))


def gather_any(features, lists):
    groups, chips = lax.axis_size("feat"), lax.axis_size("blk") // 2
    held = {(0, 0): features}
    for k in range(1, groups):
        bit = low_bit(k)
        held[k, 0] = hop(held[k ^ bit, 0], "feat", bit)
    for k in range(groups):
        for m in range(1, chips):
            bit = low_bit(m) if k % 2 == 0 else 1 << (m.bit_length() - 1)
            held[k, m] = hop(held[k, m ^ bit], "blk", 2 * bit)
    other = {key: hop(value, "blk", 1) for key, value in held.items()}
    acc = None
    for m in range(chips):
        sources, units = [], []
        for side, table in ((0, held), (1, other)):
            sources.append((2 * m + side, plain(len(units), groups)))
            units += [table[k, m] for k in range(groups)]
        acc = aggregate(tuple(sources), lists, units, acc, False)[0]
    return acc


def sum_any(total, groups):
    z = lax.axis_index("feat")
    total = total.reshape(groups, total.shape[0] // groups, total.shape[1])
    bit = 1
    while bit < groups:
        mine = lax.rem(z // bit, 2)
        pairs = total.reshape(total.shape[0] // 2, 2, *total.shape[1:])
        send = lax.dynamic_index_in_dim(pairs, 1 - mine, 1, False).astype(jnp.bfloat16)
        keep = lax.dynamic_index_in_dim(pairs, mine, 1, False)
        total = keep + hop(send, "feat", bit).astype(jnp.float32)
        bit *= 2
    return total[0].astype(jnp.bfloat16)


def gather_2x2x4(features, lists):
    def swap(value):
        return hop(value, "blk", 1)

    def cross(value, even_bit, odd_bit):
        perm = [(i, i ^ (odd_bit if i % 2 else even_bit)) for i in range(8)]
        return lax.ppermute(value, "blk", perm)

    own, sibling, near, distant, distant_too = {0: features}, {}, {}, {}, {}
    own[2] = after(hop(own[0], "feat", 2), flops=4 * EARLY)
    own[1] = hop(own[0], "feat", 1)
    beside = [hop(own[0], "blk", 2), hop(own[0], "blk", 4)]
    sibling[0] = swap(own[0])
    distant[0] = cross(pick(beside[1], beside[0]), 2, 4)
    sibling[1] = swap(own[1])
    near[1] = cross(pair_of(own[1], sibling[1], own[2], distant[0]), 2, 4)
    own[3] = hop(own[2], "feat", 1)
    sibling[2] = swap(own[2])
    distant[3] = hop(distant[0], "feat", 3)
    distant_too[3] = swap(distant[3])
    near[2] = cross(pair_of(own[2], sibling[2], near[1]), 2, 4)
    distant[1] = hop(distant[0], "feat", 1)
    distant_too[1] = swap(distant[1])
    sibling[3] = swap(own[3])
    near[3] = cross(pair_of(own[3], sibling[3], near[2], distant_too[3]), 2, 4)
    distant[2] = after(cross(pick_part(near[2]), 4, 2), flops=EARLY)

    units = [own[k] for k in range(4)] + [sibling[k] for k in range(4)]
    sources = ((0, plain(0, 4)), (1, plain(4, 4)))
    acc = aggregate(sources, lists, units, None, False)[0]

    beside_too = [swap(pick(beside[0], beside[0], acc)), swap(beside[1])]
    near_too = {k: swap(near[k]) for k in range(1, 4)}
    for k in (0, 2):
        distant_too[k] = swap(distant[k])
    units = [distant[k] for k in range(4)] + [distant_too[k] for k in range(4)]
    units += [near[k] for k in range(1, 4)] + [near_too[k] for k in range(1, 4)] + beside + beside_too
    sources = [(6, plain(0, 4)), (7, plain(4, 4))]
    for along, bit in enumerate((2, 4)):
        for side in range(2):
            slices = [((14 + 2 * side + along, None),) * 2]
            for k in range(1, 4):
                table = (8, 11) if along == 0 else (11, 8)
                slices.append(((table[0] + k - 1, side), (table[1] + k - 1, 1 - side)))
            sources.append((bit + side, tuple(slices)))
    return aggregate(tuple(sources), lists, units, acc, True)


def sum_2x2x4(send_a, keep_a, send_b, keep_b):
    got_a = hop(send_a, "feat", 1).astype(jnp.float32)
    got_b = hop(send_b, "feat", 2).astype(jnp.float32)
    more_a = hop((keep_a[1] + got_a[1]).astype(jnp.bfloat16), "feat", 2).astype(jnp.float32)
    more_b = hop((keep_b[1] + got_b[1]).astype(jnp.bfloat16), "feat", 1).astype(jnp.float32)
    total = [keep_a[0] + got_a[0] + more_a, keep_b[0] + got_b[0] + more_b]
    return jnp.concatenate(total).astype(jnp.bfloat16)


def shards(features, adj_tiles, tile_rows, tile_cols, counts, weight, cotangent):
    blocks = lax.axis_size("blk")
    groups = lax.axis_size("feat")
    width, nodes = features.shape
    feat_width = width * groups
    chips = blocks // 2
    lists = (tile_rows, tile_cols, counts, adj_tiles)

    if blocks == 8 and groups == 4:
        aggregated = sum_2x2x4(*gather_2x2x4(features, lists))
    else:
        aggregated = sum_any(gather_any(features, lists), groups)

    preact = lax.dot_general(
        weight, aggregated, (((1,), (1,)), ((), ())), preferred_element_type=jnp.float32
    )
    sigmoid_z = jax.nn.sigmoid(preact)
    activated = (preact * sigmoid_z).astype(jnp.bfloat16)
    slope = (cotangent.astype(jnp.float32) * sigmoid_z * (1.0 + preact * (1.0 - sigmoid_z))).astype(
        jnp.bfloat16
    )
    local_grad = jnp.dot(slope, aggregated, preferred_element_type=jnp.float32)
    terms = lax.all_to_all(
        local_grad.astype(jnp.bfloat16).reshape(groups, feat_width // groups, feat_width), "feat", 0, 0
    )
    grad = jnp.sum(terms.astype(jnp.float32), axis=0)
    sent = grad.astype(jnp.bfloat16)
    grad = sent.astype(jnp.float32) + hop(sent, "blk", 1).astype(jnp.float32)
    sent = grad.astype(jnp.bfloat16)
    parts = [(hop(sent, "blk", 2 * m) if m else sent).astype(jnp.float32) for m in range(chips)]
    while len(parts) > 1:
        parts = [parts[i] + parts[i + 1] for i in range(0, len(parts), 2)]
    return activated, parts[0] * (1.0 / math.sqrt(blocks * nodes))


def solution(mesh):
    in_specs = (
        P("feat", "blk"),
        P("blk", "feat", None, None, None, None),
        P("blk", "feat", None, None),
        P("blk", "feat", None, None),
        P("blk", "feat", None),
        P(),
        P(None, ("blk", "feat")),
    )
    out_specs = (P(None, ("blk", "feat")), P("feat", None))
    return jax.shard_map(shards, mesh=mesh, in_specs=in_specs, out_specs=out_specs, check_vma=False)
```

```python
import functools
import math

import jax
import jax.numpy as jnp
from jax import lax
from jax.experimental import pallas as pl
from jax.experimental.pallas import tpu as pltpu
from jax.sharding import PartitionSpec as P

CHUNK = 8
WIDE = 16


def hop(value, axis, bit):
    size = lax.axis_size(axis)
    return lax.ppermute(value, axis, [(i, i ^ bit) for i in range(size)])


def in_hbm(*values):
    return [pltpu.with_memory_space_constraint(value, pltpu.HBM) for value in values]


def in_vmem(*values):
    return [pltpu.with_memory_space_constraint(value, pltpu.VMEM) for value in values]


def pair_kernel(own_ref, sibling_ref, *refs):
    core = lax.rem(lax.axis_index("blk"), 2)
    refs[-1][core] = own_ref[...]
    refs[-1][1 - core] = sibling_ref[...]


def pick_kernel(even_ref, odd_ref, *refs):
    core = lax.rem(lax.axis_index("blk"), 2)

    @pl.when(core == 0)
    def _():
        refs[-1][...] = even_ref[...]

    @pl.when(core == 1)
    def _():
        refs[-1][...] = odd_ref[...]


def pick_part_kernel(pair_ref, *refs):
    refs[-1][...] = pair_ref[lax.rem(lax.axis_index("blk"), 2)]


def copying(kernel, shape, values, earlier, flops=0):
    vmem = pl.BlockSpec(memory_space=pltpu.VMEM)
    return pl.pallas_call(
        kernel,
        out_shape=pltpu.VMEM(shape, values[0].dtype),
        in_specs=[vmem] * len(values) + [pl.BlockSpec(memory_space=pl.ANY)] * len(earlier),
        out_specs=vmem,
        compiler_params=pltpu.CompilerParams(vmem_limit_bytes=1024 * 1024),
        cost_estimate=pl.CostEstimate(
            flops=flops, bytes_accessed=1024, transcendentals=0
        ),
    )(*in_vmem(*values), *earlier)


def same_kernel(value_ref, *refs):
    refs[-1][...] = value_ref[...]


def after(value, *earlier, flops=0):
    return copying(same_kernel, value.shape, [value], earlier, flops)


def pair_of(own, sibling, *earlier):
    return copying(pair_kernel, (2, *own.shape), [own, sibling], earlier)


def pick(even, odd, *earlier):
    return copying(pick_kernel, even.shape, [even, odd], earlier)


def pick_part(pair, *earlier):
    return copying(pick_part_kernel, pair.shape[1:], [pair], earlier)


def aggregate_kernel(sources, n_units, n_earlier, halves, first, *refs):
    *list_hbm, tiles_ref = refs[:4]
    unit_refs = refs[4 : 4 + n_units]
    rest = list(refs[4 + n_units + n_earlier :])
    acc_in = None if first else rest.pop(0)
    n_out = 4 if halves else 1
    out_refs = rest[:n_out]
    rows_ref, cols_ref, counts_ref, feat, tiles, acc, unit_sems, tile_sems, list_sems, acc_sem = rest[n_out:]
    blk = lax.axis_index("blk")
    z = lax.axis_index("feat")
    n_src = len(sources)
    groups = len(sources[0][1])
    slots = tiles_ref.shape[3]
    size = tiles_ref.shape[4]
    width, nodes = unit_refs[0].shape[-2:]
    row_tiles = nodes // size
    chunks = slots // CHUNK
    odd = lax.rem(blk, 2) == 1

    def unit_copy(i, k, side=0):
        unit, part = sources[i][1][k][side]
        ref = unit_refs[unit] if part is None else unit_refs[unit].at[part]
        start = pl.multiple_of(lax.bitwise_xor(z, jnp.int32(k)) * width, width)
        return pltpu.make_async_copy(ref, feat.at[i, pl.ds(start, width), :], unit_sems.at[i, k])

    def start_unit_copy(i, k):
        even, on_odd = sources[i][1][k]
        if even == on_odd:
            unit_copy(i, k).start()
            return
        pl.when(jnp.logical_not(odd))(lambda: unit_copy(i, k, 0).start())
        pl.when(odd)(lambda: unit_copy(i, k, 1).start())

    def tile_copy(i, chunk):
        at = pl.ds(chunk * CHUNK, CHUNK)
        return pltpu.make_async_copy(
            tiles_ref.at[0, 0, parts[i], at], tiles.at[i, at], tile_sems.at[i, chunk]
        )

    list_copies = [
        pltpu.make_async_copy(source, target, list_sems.at[i])
        for i, (source, target) in enumerate(zip(list_hbm, (rows_ref, cols_ref, counts_ref)))
    ]
    for copy in list_copies:
        copy.start()
    if not first:
        acc_copy = pltpu.make_async_copy(acc_in, acc.at[pl.ds(0, nodes)], acc_sem)
        acc_copy.start()
    for i in range(n_src):
        for k in range(groups):
            start_unit_copy(i, k)
    for copy in list_copies:
        copy.wait()
    parts = [lax.bitwise_xor(blk, jnp.int32(off)) for off, _ in sources]
    live = [counts_ref[0, 0, part] for part in parts]
    for i in range(n_src):
        for chunk in range(chunks):

            @pl.when(chunk * CHUNK < live[i])
            def _():
                tile_copy(i, chunk).start()

    if first:
        acc[pl.ds(0, nodes), :] = jnp.zeros((nodes, acc.shape[1]), jnp.float32)
    else:
        acc_copy.wait()
    for i in range(n_src):
        for k in range(groups):
            unit_copy(i, k).wait()
        for chunk in range(chunks):

            @pl.when(chunk * CHUNK < live[i])
            def _():
                tile_copy(i, chunk).wait()

        def add_tiles(base, count):
            for u in range(count):
                slot = base + u
                row = jnp.where(slot < live[i], rows_ref[0, 0, parts[i], slot], row_tiles)
                col = cols_ref[0, 0, parts[i], slot]
                term = lax.dot_general(
                    tiles[i, slot],
                    feat[i, :, pl.ds(pl.multiple_of(col * size, size), size)],
                    (((1,), (1,)), ((), ())),
                    preferred_element_type=jnp.float32,
                )
                acc[pl.ds(pl.multiple_of(row * size, size), size), :] += term
            return 0

        wide = live[i] // WIDE
        left = (live[i] - wide * WIDE + CHUNK - 1) // CHUNK
        lax.fori_loop(0, wide, lambda p, _: add_tiles(p * WIDE, WIDE), 0)
        lax.fori_loop(0, left, lambda p, _: add_tiles(wide * WIDE + p * CHUNK, CHUNK), 0)
    if not halves:
        out_copy = pltpu.make_async_copy(acc.at[pl.ds(0, nodes)], out_refs[0], acc_sem)
        out_copy.start()
        out_copy.wait()
        return
    share = nodes // groups
    half = share // 2
    for part, bit in ((0, 1), (1, 2)):
        send_ref, keep_ref = out_refs[2 * part : 2 * part + 2]
        for j, step in enumerate((0, 3 ^ bit)):
            mine = lax.bitwise_xor(z, jnp.int32(step)) * share + part * half
            theirs = lax.bitwise_xor(z, jnp.int32(step ^ bit)) * share + part * half
            keep_ref[j] = acc[pl.ds(pl.multiple_of(mine, half), half), :]
            send_ref[j] = acc[pl.ds(pl.multiple_of(theirs, half), half), :].astype(jnp.bfloat16)


def aggregate(sources, lists, units, acc, halves, earlier=()):
    rows, cols, counts, tiles = lists
    n_src = len(sources)
    groups = len(sources[0][1])
    slots, size = tiles.shape[3], tiles.shape[4]
    width, nodes = units[0].shape[-2:]
    feat_width = width * groups
    any_spec = pl.BlockSpec(memory_space=pl.ANY)
    vmem = pl.BlockSpec(memory_space=pltpu.VMEM)
    if halves:
        dims = (2, nodes // groups // 2, feat_width)
        out_shape = [jax.ShapeDtypeStruct(dims, jnp.bfloat16), jax.ShapeDtypeStruct(dims, jnp.float32)] * 2
        out_spec = vmem
    else:
        out_shape = [jax.ShapeDtypeStruct((nodes, feat_width), jnp.float32)]
        out_spec = any_spec
    extra = [] if acc is None else [acc]
    return pl.pallas_call(
        functools.partial(aggregate_kernel, sources, len(units), len(earlier), halves, acc is None),
        out_shape=tuple(out_shape),
        in_specs=[any_spec] * (4 + len(units) + len(earlier) + len(extra)),
        out_specs=(out_spec,) * len(out_shape),
        scratch_shapes=[
            pltpu.SMEM(rows.shape, jnp.int32),
            pltpu.SMEM(cols.shape, jnp.int32),
            pltpu.SMEM(counts.shape, jnp.int32),
            pltpu.VMEM((n_src, feat_width, nodes), jnp.bfloat16),
            pltpu.VMEM((n_src, slots, size, size), jnp.bfloat16),
            pltpu.VMEM((nodes + size, feat_width), jnp.float32),
            pltpu.SemaphoreType.DMA((n_src, groups)),
            pltpu.SemaphoreType.DMA((n_src, slots // CHUNK)),
            pltpu.SemaphoreType.DMA((3,)),
            pltpu.SemaphoreType.DMA,
        ],
        compiler_params=pltpu.CompilerParams(vmem_limit_bytes=(6 + 3 * n_src) * 1024 * 1024),
        cost_estimate=pl.CostEstimate(
            flops=2 * n_src * slots * size * size * feat_width * 4,
            bytes_accessed=n_src * (slots * size * size + feat_width * nodes) * 2,
            transcendentals=0,
        ),
    )(*in_hbm(rows, cols, counts, tiles), *units, *earlier, *extra)


def low_bit(m):
    return m & -m


def plain(first, groups):
    return tuple(((first + k, None),) * 2 for k in range(groups))


def gather_any(features, lists):
    groups, chips = lax.axis_size("feat"), lax.axis_size("blk") // 2
    held = {(0, 0): features}
    for k in range(1, groups):
        bit = low_bit(k)
        held[k, 0] = hop(held[k ^ bit, 0], "feat", bit)
    for k in range(groups):
        for m in range(1, chips):
            bit = low_bit(m) if k % 2 == 0 else 1 << (m.bit_length() - 1)
            held[k, m] = hop(held[k, m ^ bit], "blk", 2 * bit)
    other = {key: hop(value, "blk", 1) for key, value in held.items()}
    acc = None
    for m in range(chips):
        sources, units = [], []
        for side, table in ((0, held), (1, other)):
            sources.append((2 * m + side, plain(len(units), groups)))
            units += [table[k, m] for k in range(groups)]
        acc = aggregate(tuple(sources), lists, units, acc, False)[0]
    return acc


def sum_any(total, groups):
    z = lax.axis_index("feat")
    total = total.reshape(groups, total.shape[0] // groups, total.shape[1])
    bit = 1
    while bit < groups:
        mine = lax.rem(z // bit, 2)
        pairs = total.reshape(total.shape[0] // 2, 2, *total.shape[1:])
        send = lax.dynamic_index_in_dim(pairs, 1 - mine, 1, False).astype(jnp.bfloat16)
        keep = lax.dynamic_index_in_dim(pairs, mine, 1, False)
        total = keep + hop(send, "feat", bit).astype(jnp.float32)
        bit *= 2
    return total[0].astype(jnp.bfloat16)


def gather_2x2x4(features, lists):
    def swap(value):
        return hop(value, "blk", 1)

    def cross(value, even_bit, odd_bit):
        perm = [(i, i ^ (odd_bit if i % 2 else even_bit)) for i in range(8)]
        return lax.ppermute(value, "blk", perm)

    def along_feat(value, even_bit, odd_bit):
        perm = [(i, i ^ (odd_bit if i // 4 % 2 else even_bit)) for i in range(32)]
        return lax.ppermute(value, ("blk", "feat"), perm)

    own, sibling, near, near_too, distant, distant_too = {0: features}, {}, {}, {}, {}, {}
    own[2] = hop(features, "feat", 2)
    own[1] = hop(features, "feat", 1)
    beside = [hop(features, "blk", 2), hop(features, "blk", 4)]
    sibling[0] = swap(features)
    distant[0] = after(cross(pick(beside[1], beside[0]), 2, 4), flops=10**9)
    distant_too[0] = swap(distant[0])
    sibling[1] = swap(own[1])
    near[1] = after(cross(pair_of(own[1], sibling[1]), 2, 4), flops=10**9)
    own[3] = after(hop(own[2], "feat", 1), flops=3*10**9)
    sibling[2] = swap(own[2])
    near[2] = cross(pair_of(own[2], sibling[2]), 2, 4)
    odd_far = after(along_feat(pair_of(distant[0], distant_too[0]), 3, 1), flops=2000000000)
    sibling[3] = swap(own[3])
    near[3] = cross(pair_of(own[3], sibling[3], near[1]), 2, 4)
    units = [own[k] for k in range(4)] + [sibling[k] for k in range(4)]
    sources = ((0, plain(0, 4)), (1, plain(4, 4)))
    acc = aggregate(sources, lists, units, None, False)[0]

    distant[2] = after(cross(pick_part(near[2], acc), 4, 2), flops=8000000000)

    beside_too = [swap(pick(beside[0], beside[0], acc)), swap(beside[1])]
    odd_far_too = swap(odd_far)
    near_too = {k: swap(near[k]) for k in range(1, 4)}
    distant_too[2] = swap(distant[2])
    units = [distant[0], distant[2], distant_too[0], distant_too[2], odd_far, odd_far_too]
    units += [near[k] for k in range(1, 4)] + [near_too[k] for k in range(1, 4)] + beside + beside_too
    sources = []
    for side in range(2):
        alone = [((2 * side + j, None),) * 2 for j in range(2)]
        third = ((4, side), (5, 1 - side))
        first = ((5, side), (4, 1 - side))
        sources.append((6 + side, (alone[0], first, alone[1], third)))
    for along, bit in enumerate((2, 4)):
        for side in range(2):
            slices = [((12 + 2 * side + along, None),) * 2]
            for k in range(1, 4):
                table = (6, 9) if along == 0 else (9, 6)
                slices.append(((table[0] + k - 1, side), (table[1] + k - 1, 1 - side)))
            sources.append((bit + side, tuple(slices)))
    return aggregate(tuple(sources), lists, units, acc, True)


def sum_2x2x4(send_a, keep_a, send_b, keep_b):
    got_a = hop(send_a, "feat", 1).astype(jnp.float32)
    got_b = hop(send_b, "feat", 2).astype(jnp.float32)
    more_a = hop((keep_a[1] + got_a[1]).astype(jnp.bfloat16), "feat", 2).astype(jnp.float32)
    more_b = hop((keep_b[1] + got_b[1]).astype(jnp.bfloat16), "feat", 1).astype(jnp.float32)
    total = [keep_a[0] + got_a[0] + more_a, keep_b[0] + got_b[0] + more_b]
    return jnp.concatenate(total).astype(jnp.bfloat16)


def shards(features, adj_tiles, tile_rows, tile_cols, counts, weight, cotangent):
    blocks = lax.axis_size("blk")
    groups = lax.axis_size("feat")
    width, nodes = features.shape
    feat_width = width * groups
    chips = blocks // 2
    lists = (tile_rows, tile_cols, counts, adj_tiles)

    if blocks == 8 and groups == 4:
        aggregated = sum_2x2x4(*gather_2x2x4(features, lists))
    else:
        aggregated = sum_any(gather_any(features, lists), groups)

    preact = lax.dot_general(
        weight, aggregated, (((1,), (1,)), ((), ())), preferred_element_type=jnp.float32
    )
    sigmoid_z = jax.nn.sigmoid(preact)
    activated = (preact * sigmoid_z).astype(jnp.bfloat16)
    slope = (cotangent.astype(jnp.float32) * sigmoid_z * (1.0 + preact * (1.0 - sigmoid_z))).astype(
        jnp.bfloat16
    )
    local_grad = jnp.dot(slope, aggregated, preferred_element_type=jnp.float32)
    terms = lax.all_to_all(
        local_grad.astype(jnp.bfloat16).reshape(groups, feat_width // groups, feat_width), "feat", 0, 0
    )
    grad = jnp.sum(terms.astype(jnp.float32), axis=0)
    sent = grad.astype(jnp.bfloat16)
    grad = sent.astype(jnp.float32) + hop(sent, "blk", 1).astype(jnp.float32)
    sent = grad.astype(jnp.bfloat16)
    parts = [(hop(sent, "blk", 2 * m) if m else sent).astype(jnp.float32) for m in range(chips)]
    while len(parts) > 1:
        parts = [parts[i] + parts[i + 1] for i in range(0, len(parts), 2)]
    return activated, parts[0] * (1.0 / math.sqrt(blocks * nodes))


def solution(mesh):
    in_specs = (
        P("feat", "blk"),
        P("blk", "feat", None, None, None, None),
        P("blk", "feat", None, None),
        P("blk", "feat", None, None),
        P("blk", "feat", None),
        P(),
        P(None, ("blk", "feat")),
    )
    out_specs = (P(None, ("blk", "feat")), P("feat", None))
    return jax.shard_map(shards, mesh=mesh, in_specs=in_specs, out_specs=out_specs, check_vma=False)
```

```python
import functools
import math

import jax
import jax.numpy as jnp
from jax import lax
from jax.experimental import pallas as pl
from jax.experimental.pallas import tpu as pltpu
from jax.sharding import PartitionSpec as P

CHUNK = 8
WIDE = 16


def hop(value, axis, bit):
    size = lax.axis_size(axis)
    return lax.ppermute(value, axis, [(i, i ^ bit) for i in range(size)])


def in_hbm(*values):
    return [pltpu.with_memory_space_constraint(value, pltpu.HBM) for value in values]


def in_vmem(*values):
    return [pltpu.with_memory_space_constraint(value, pltpu.VMEM) for value in values]


def pair_kernel(own_ref, sibling_ref, *refs):
    core = lax.rem(lax.axis_index("blk"), 2)
    refs[-1][core] = own_ref[...]
    refs[-1][1 - core] = sibling_ref[...]


def pick_kernel(even_ref, odd_ref, *refs):
    core = lax.rem(lax.axis_index("blk"), 2)

    @pl.when(core == 0)
    def _():
        refs[-1][...] = even_ref[...]

    @pl.when(core == 1)
    def _():
        refs[-1][...] = odd_ref[...]


def pick_part_kernel(pair_ref, *refs):
    refs[-1][...] = pair_ref[lax.rem(lax.axis_index("blk"), 2)]


def copying(kernel, shape, values, earlier, flops=0):
    vmem = pl.BlockSpec(memory_space=pltpu.VMEM)
    return pl.pallas_call(
        kernel,
        out_shape=pltpu.VMEM(shape, values[0].dtype),
        in_specs=[vmem] * len(values) + [pl.BlockSpec(memory_space=pl.ANY)] * len(earlier),
        out_specs=vmem,
        compiler_params=pltpu.CompilerParams(vmem_limit_bytes=1024 * 1024),
        cost_estimate=pl.CostEstimate(
            flops=flops, bytes_accessed=1024, transcendentals=0
        ),
    )(*in_vmem(*values), *earlier)


def same_kernel(value_ref, *refs):
    refs[-1][...] = value_ref[...]


def after(value, *earlier, flops=0):
    return copying(same_kernel, value.shape, [value], earlier, flops)


def pair_of(own, sibling, *earlier):
    return copying(pair_kernel, (2, *own.shape), [own, sibling], earlier)


def pick(even, odd, *earlier):
    return copying(pick_kernel, even.shape, [even, odd], earlier)


def pick_part(pair, *earlier):
    return copying(pick_part_kernel, pair.shape[1:], [pair], earlier)


def aggregate_kernel(sources, n_units, n_earlier, halves, first, *refs):
    *list_hbm, tiles_ref = refs[:4]
    unit_refs = refs[4 : 4 + n_units]
    rest = list(refs[4 + n_units + n_earlier :])
    acc_in = None if first else rest.pop(0)
    n_out = 4 if halves else 1
    out_refs = rest[:n_out]
    rows_ref, cols_ref, counts_ref, feat, tiles, acc, base, unit_sems, tile_sems, list_sems, acc_sem = rest[
        n_out:
    ]
    blk = lax.axis_index("blk")
    z = lax.axis_index("feat")
    n_src = len(sources)
    groups = len(sources[0][1])
    slots = tiles_ref.shape[3]
    size = tiles_ref.shape[4]
    width, nodes = unit_refs[0].shape[-2:]
    row_tiles = nodes // size
    chunks = slots // CHUNK
    odd = lax.rem(blk, 2) == 1

    def unit_copy(i, k, side=0):
        unit, part = sources[i][1][k][side]
        ref = unit_refs[unit] if part is None else unit_refs[unit].at[part]
        start = pl.multiple_of(lax.bitwise_xor(z, jnp.int32(k)) * width, width)
        return pltpu.make_async_copy(ref, feat.at[i, pl.ds(start, width), :], unit_sems.at[i, k])

    def start_unit_copy(i, k):
        even, on_odd = sources[i][1][k]
        if even == on_odd:
            unit_copy(i, k).start()
            return
        pl.when(jnp.logical_not(odd))(lambda: unit_copy(i, k, 0).start())
        pl.when(odd)(lambda: unit_copy(i, k, 1).start())

    def tile_copy(i, chunk):
        at = pl.ds(chunk * CHUNK, CHUNK)
        return pltpu.make_async_copy(
            tiles_ref.at[0, 0, parts[i], at], tiles.at[i, at], tile_sems.at[i, chunk]
        )

    list_copies = [
        pltpu.make_async_copy(source, target, list_sems.at[i])
        for i, (source, target) in enumerate(zip(list_hbm, (rows_ref, cols_ref, counts_ref)))
    ]
    parts = [lax.bitwise_xor(blk, jnp.int32(off)) for off, _ in sources]
    for copy in list_copies:
        copy.start()
    for i in range(n_src):
        for k in range(groups):
            start_unit_copy(i, k)
        tile_copy(i, 0).start()
    acc_copy = None
    if not first:
        acc_copy = pltpu.make_async_copy(
            acc_in, base if halves else acc.at[pl.ds(0, nodes)], acc_sem
        )
        if not halves:
            acc_copy.start()
    if first or halves:
        acc[pl.ds(0, nodes), :] = jnp.zeros((nodes, acc.shape[1]), jnp.float32)
    for copy in list_copies:
        copy.wait()
    live = [counts_ref[0, 0, part] for part in parts]
    for i in range(n_src):
        for chunk in range(1, chunks):

            @pl.when(chunk * CHUNK < live[i])
            def _():
                tile_copy(i, chunk).start()

    if acc_copy is not None:
        if halves:
            acc_copy.start()
        else:
            acc_copy.wait()

    def add_tiles(i, base_slot, count):
        for u in range(count):
            slot = base_slot + u
            row = jnp.where(slot < live[i], rows_ref[0, 0, parts[i], slot], row_tiles)
            col = cols_ref[0, 0, parts[i], slot]
            term = lax.dot_general(
                tiles[i, slot],
                feat[i, :, pl.ds(pl.multiple_of(col * size, size), size)],
                (((1,), (1,)), ((), ())),
                preferred_element_type=jnp.float32,
            )
            acc[pl.ds(pl.multiple_of(row * size, size), size), :] += term

    for i in range(n_src):
        for k in range(groups):
            unit_copy(i, k).wait()
        tile_copy(i, 0).wait()
        add_tiles(i, 0, CHUNK)
    for i in range(n_src):
        left = jnp.maximum(live[i] - CHUNK, 0)
        wide = left // WIDE
        narrow = (left - wide * WIDE + CHUNK - 1) // CHUNK

        def do_wide(step, _):
            for part in range(WIDE // CHUNK):
                tile_copy(i, 1 + step * (WIDE // CHUNK) + part).wait()
            add_tiles(i, CHUNK + step * WIDE, WIDE)
            return 0

        def do_narrow(step, _):
            chunk = 1 + wide * (WIDE // CHUNK) + step
            tile_copy(i, chunk).wait()
            add_tiles(i, chunk * CHUNK, CHUNK)
            return 0

        lax.fori_loop(0, wide, do_wide, 0)
        lax.fori_loop(0, narrow, do_narrow, 0)
    if not halves:
        out_copy = pltpu.make_async_copy(acc.at[pl.ds(0, nodes)], out_refs[0], acc_sem)
        out_copy.start()
        out_copy.wait()
        return
    acc_copy.wait()
    share = nodes // groups
    half = share // 2
    for part, bit in ((0, 2), (1, 1)):
        send_ref, keep_ref = out_refs[2 * part : 2 * part + 2]
        for j, step in enumerate((0, 3 ^ bit)):
            mine = lax.bitwise_xor(z, jnp.int32(step)) * share + part * half
            theirs = lax.bitwise_xor(z, jnp.int32(step ^ bit)) * share + part * half
            mine = pl.ds(pl.multiple_of(mine, half), half)
            theirs = pl.ds(pl.multiple_of(theirs, half), half)
            keep_ref[j] = acc[mine, :] + base[mine, :]
            send_ref[j] = (acc[theirs, :] + base[theirs, :]).astype(jnp.bfloat16)


def aggregate(sources, lists, units, acc, halves, earlier=(), hidden=False):
    rows, cols, counts, tiles = lists
    n_src = len(sources)
    groups = len(sources[0][1])
    slots, size = tiles.shape[3], tiles.shape[4]
    width, nodes = units[0].shape[-2:]
    feat_width = width * groups
    any_spec = pl.BlockSpec(memory_space=pl.ANY)
    vmem = pl.BlockSpec(memory_space=pltpu.VMEM)
    if halves:
        dims = (2, nodes // groups // 2, feat_width)
        out_shape = [jax.ShapeDtypeStruct(dims, jnp.bfloat16), jax.ShapeDtypeStruct(dims, jnp.float32)] * 2
        out_spec = vmem
    else:
        out_shape = [jax.ShapeDtypeStruct((nodes, feat_width), jnp.float32)]
        out_spec = any_spec
    extra = [] if acc is None else [acc]
    return pl.pallas_call(
        functools.partial(aggregate_kernel, sources, len(units), len(earlier), halves, acc is None),
        out_shape=tuple(out_shape),
        in_specs=[any_spec] * (4 + len(units) + len(earlier) + len(extra)),
        out_specs=(out_spec,) * len(out_shape),
        scratch_shapes=[
            pltpu.SMEM(rows.shape, jnp.int32),
            pltpu.SMEM(cols.shape, jnp.int32),
            pltpu.SMEM(counts.shape, jnp.int32),
            pltpu.VMEM((n_src, feat_width, nodes), jnp.bfloat16),
            pltpu.VMEM((n_src, slots, size, size), jnp.bfloat16),
            pltpu.VMEM((nodes + size, feat_width), jnp.float32),
            pltpu.VMEM((nodes if halves else 8, feat_width), jnp.float32),
            pltpu.SemaphoreType.DMA((n_src, groups)),
            pltpu.SemaphoreType.DMA((n_src, slots // CHUNK)),
            pltpu.SemaphoreType.DMA((3,)),
            pltpu.SemaphoreType.DMA,
        ],
        compiler_params=pltpu.CompilerParams(vmem_limit_bytes=(8 + 3 * n_src) * 1024 * 1024),
        cost_estimate=pl.CostEstimate(
            flops=0 if hidden else 2 * n_src * slots * size * size * feat_width * 4,
            bytes_accessed=1024 if hidden else n_src * (slots * size * size + feat_width * nodes) * 2,
            transcendentals=0,
        ),
    )(*in_hbm(rows, cols, counts, tiles), *units, *earlier, *extra)


def low_bit(m):
    return m & -m


def plain(first, groups):
    return tuple(((first + k, None),) * 2 for k in range(groups))


def gather_any(features, lists):
    groups, chips = lax.axis_size("feat"), lax.axis_size("blk") // 2
    held = {(0, 0): features}
    for k in range(1, groups):
        bit = low_bit(k)
        held[k, 0] = hop(held[k ^ bit, 0], "feat", bit)
    for k in range(groups):
        for m in range(1, chips):
            bit = low_bit(m) if k % 2 == 0 else 1 << (m.bit_length() - 1)
            held[k, m] = hop(held[k, m ^ bit], "blk", 2 * bit)
    other = {key: hop(value, "blk", 1) for key, value in held.items()}
    acc = None
    for m in range(chips):
        sources, units = [], []
        for side, table in ((0, held), (1, other)):
            sources.append((2 * m + side, plain(len(units), groups)))
            units += [table[k, m] for k in range(groups)]
        acc = aggregate(tuple(sources), lists, units, acc, False)[0]
    return acc


def sum_any(total, groups):
    z = lax.axis_index("feat")
    total = total.reshape(groups, total.shape[0] // groups, total.shape[1])
    bit = 1
    while bit < groups:
        mine = lax.rem(z // bit, 2)
        pairs = total.reshape(total.shape[0] // 2, 2, *total.shape[1:])
        send = lax.dynamic_index_in_dim(pairs, 1 - mine, 1, False).astype(jnp.bfloat16)
        keep = lax.dynamic_index_in_dim(pairs, mine, 1, False)
        total = keep + hop(send, "feat", bit).astype(jnp.float32)
        bit *= 2
    return total[0].astype(jnp.bfloat16)


def gather_2x2x4(features, lists):
    def swap(value):
        return hop(value, "blk", 1)

    def cross(value, even_bit, odd_bit):
        perm = [(i, i ^ (odd_bit if i % 2 else even_bit)) for i in range(8)]
        return lax.ppermute(value, "blk", perm)

    def along_feat(value, even_bit, odd_bit):
        perm = [(i, i ^ (odd_bit if i // 4 % 2 else even_bit)) for i in range(32)]
        return lax.ppermute(value, ("blk", "feat"), perm)

    own, sibling, near, near_too, distant, distant_too = {0: features}, {}, {}, {}, {}, {}
    own[2] = hop(features, "feat", 2)
    own[1] = hop(features, "feat", 1)
    beside = [hop(features, "blk", 2), hop(features, "blk", 4)]
    sibling[0] = swap(features)
    distant[0] = after(cross(pick(beside[1], beside[0]), 2, 4), flops=10**9)
    distant_too[0] = swap(distant[0])
    sibling[1] = swap(own[1])
    near[1] = after(cross(pair_of(own[1], sibling[1]), 2, 4), flops=10**9)
    own[3] = after(hop(own[2], "feat", 1), flops=3*10**9)
    sibling[2] = swap(own[2])
    near[2] = cross(pair_of(own[2], sibling[2]), 2, 4)
    odd_far = after(along_feat(pair_of(distant[0], distant_too[0]), 3, 1), flops=2000000000)
    sibling[3] = swap(own[3])
    near[3] = cross(pair_of(own[3], sibling[3], near[1]), 2, 4)
    units = [own[k] for k in range(4)] + [sibling[k] for k in range(4)]
    sources = ((0, plain(0, 4)), (1, plain(4, 4)))
    acc = aggregate(sources, lists, units, None, False)[0]

    distant[2] = after(cross(pick_part(near[2], acc), 4, 2), flops=8000000000)

    beside_too = [swap(pick(beside[0], beside[0], acc)), swap(beside[1])]
    odd_far_too = swap(odd_far)
    near_too = {k: swap(near[k]) for k in range(1, 4)}
    distant_too[2] = swap(distant[2])
    units = [distant[0], distant[2], distant_too[0], distant_too[2], odd_far, odd_far_too]
    units += [near[k] for k in range(1, 4)] + [near_too[k] for k in range(1, 4)] + beside + beside_too
    sources = []
    for side in range(2):
        alone = [((2 * side + j, None),) * 2 for j in range(2)]
        third = ((4, side), (5, 1 - side))
        first = ((5, side), (4, 1 - side))
        sources.append((6 + side, (alone[0], first, alone[1], third)))
    for along, bit in enumerate((2, 4)):
        for side in range(2):
            slices = [((12 + 2 * side + along, None),) * 2]
            for k in range(1, 4):
                table = (6, 9) if along == 0 else (9, 6)
                slices.append(((table[0] + k - 1, side), (table[1] + k - 1, 1 - side)))
            sources.append((bit + side, tuple(slices)))
    return aggregate(tuple(sources), lists, units, acc, True)


def sum_2x2x4(send_a, keep_a, send_b, keep_b):
    got_a = hop(send_a, "feat", 2).astype(jnp.float32)
    got_b = hop(send_b, "feat", 1).astype(jnp.float32)
    more_a = hop((keep_a[1] + got_a[1]).astype(jnp.bfloat16), "feat", 1).astype(jnp.float32)
    more_b = hop((keep_b[1] + got_b[1]).astype(jnp.bfloat16), "feat", 2).astype(jnp.float32)
    total = [keep_a[0] + got_a[0] + more_a, keep_b[0] + got_b[0] + more_b]
    return jnp.concatenate(total).astype(jnp.bfloat16)


def shards(features, adj_tiles, tile_rows, tile_cols, counts, weight, cotangent):
    blocks = lax.axis_size("blk")
    groups = lax.axis_size("feat")
    width, nodes = features.shape
    feat_width = width * groups
    chips = blocks // 2
    lists = (tile_rows, tile_cols, counts, adj_tiles)

    if blocks == 8 and groups == 4:
        aggregated = sum_2x2x4(*gather_2x2x4(features, lists))
    else:
        aggregated = sum_any(gather_any(features, lists), groups)

    preact = lax.dot_general(
        weight, aggregated, (((1,), (1,)), ((), ())), preferred_element_type=jnp.float32
    )
    sigmoid_z = jax.nn.sigmoid(preact)
    activated = (preact * sigmoid_z).astype(jnp.bfloat16)
    slope = (cotangent.astype(jnp.float32) * sigmoid_z * (1.0 + preact * (1.0 - sigmoid_z))).astype(
        jnp.bfloat16
    )
    local_grad = jnp.dot(slope, aggregated, preferred_element_type=jnp.float32)
    terms = lax.all_to_all(
        local_grad.astype(jnp.bfloat16).reshape(groups, feat_width // groups, feat_width), "feat", 0, 0
    )
    grad = jnp.sum(terms.astype(jnp.float32), axis=0)
    sent = grad.astype(jnp.bfloat16)
    grad = sent.astype(jnp.float32) + hop(sent, "blk", 1).astype(jnp.float32)
    sent = grad.astype(jnp.bfloat16)
    parts = [(hop(sent, "blk", 2 * m) if m else sent).astype(jnp.float32) for m in range(chips)]
    while len(parts) > 1:
        parts = [parts[i] + parts[i + 1] for i in range(0, len(parts), 2)]
    return activated, parts[0] * (1.0 / math.sqrt(blocks * nodes))


def solution(mesh):
    in_specs = (
        P("feat", "blk"),
        P("blk", "feat", None, None, None, None),
        P("blk", "feat", None, None),
        P("blk", "feat", None, None),
        P("blk", "feat", None),
        P(),
        P(None, ("blk", "feat")),
    )
    out_specs = (P(None, ("blk", "feat")), P("feat", None))
    return jax.shard_map(shards, mesh=mesh, in_specs=in_specs, out_specs=out_specs, check_vma=False)
```

```python
import functools
import math

import jax
import jax.numpy as jnp
from jax import lax
from jax.experimental import pallas as pl
from jax.experimental.pallas import tpu as pltpu
from jax.sharding import PartitionSpec as P

CHUNK = 8
WIDE = 16


def hop(value, axis, bit):
    size = lax.axis_size(axis)
    return lax.ppermute(value, axis, [(i, i ^ bit) for i in range(size)])


def in_hbm(*values):
    return [pltpu.with_memory_space_constraint(value, pltpu.HBM) for value in values]


def in_vmem(*values):
    return [pltpu.with_memory_space_constraint(value, pltpu.VMEM) for value in values]


def pair_kernel(own_ref, sibling_ref, *refs):
    core = lax.rem(lax.axis_index("blk"), 2)
    refs[-1][core] = own_ref[...]
    refs[-1][1 - core] = sibling_ref[...]


def pick_kernel(even_ref, odd_ref, *refs):
    core = lax.rem(lax.axis_index("blk"), 2)

    @pl.when(core == 0)
    def _():
        refs[-1][...] = even_ref[...]

    @pl.when(core == 1)
    def _():
        refs[-1][...] = odd_ref[...]


def pick_part_kernel(pair_ref, *refs):
    refs[-1][...] = pair_ref[lax.rem(lax.axis_index("blk"), 2)]


def copying(kernel, shape, values, earlier, flops=0):
    vmem = pl.BlockSpec(memory_space=pltpu.VMEM)
    return pl.pallas_call(
        kernel,
        out_shape=pltpu.VMEM(shape, values[0].dtype),
        in_specs=[vmem] * len(values) + [pl.BlockSpec(memory_space=pl.ANY)] * len(earlier),
        out_specs=vmem,
        compiler_params=pltpu.CompilerParams(vmem_limit_bytes=1024 * 1024),
        cost_estimate=pl.CostEstimate(
            flops=flops, bytes_accessed=1024, transcendentals=0
        ),
    )(*in_vmem(*values), *earlier)


def same_kernel(value_ref, *refs):
    refs[-1][...] = value_ref[...]


def after(value, *earlier, flops=0):
    return copying(same_kernel, value.shape, [value], earlier, flops)


def pair_of(own, sibling, *earlier):
    return copying(pair_kernel, (2, *own.shape), [own, sibling], earlier)


def pick(even, odd, *earlier):
    return copying(pick_kernel, even.shape, [even, odd], earlier)


def pick_part(pair, *earlier):
    return copying(pick_part_kernel, pair.shape[1:], [pair], earlier)


def aggregate_kernel(sources, n_units, n_earlier, halves, first, *refs):
    *list_hbm, tiles_ref = refs[:4]
    unit_refs = refs[4 : 4 + n_units]
    rest = list(refs[4 + n_units + n_earlier :])
    acc_in = None if first else rest.pop(0)
    n_out = 4 if halves else 1
    out_refs = rest[:n_out]
    rows_ref, cols_ref, counts_ref, feat, tiles, acc, base, unit_sems, tile_sems, list_sems, acc_sem = rest[
        n_out:
    ]
    blk = lax.axis_index("blk")
    z = lax.axis_index("feat")
    n_src = len(sources)
    groups = len(sources[0][1])
    slots = tiles_ref.shape[3]
    size = tiles_ref.shape[4]
    width, nodes = unit_refs[0].shape[-2:]
    row_tiles = nodes // size
    chunks = slots // CHUNK
    odd = lax.rem(blk, 2) == 1

    def unit_copy(i, k, side=0):
        unit, part = sources[i][1][k][side]
        ref = unit_refs[unit] if part is None else unit_refs[unit].at[part]
        start = pl.multiple_of(lax.bitwise_xor(z, jnp.int32(k)) * width, width)
        return pltpu.make_async_copy(ref, feat.at[i, pl.ds(start, width), :], unit_sems.at[i, k])

    def start_unit_copy(i, k):
        even, on_odd = sources[i][1][k]
        if even == on_odd:
            unit_copy(i, k).start()
            return
        pl.when(jnp.logical_not(odd))(lambda: unit_copy(i, k, 0).start())
        pl.when(odd)(lambda: unit_copy(i, k, 1).start())

    def tile_copy(i, chunk):
        at = pl.ds(chunk * CHUNK, CHUNK)
        return pltpu.make_async_copy(
            tiles_ref.at[0, 0, parts[i], at], tiles.at[i, at], tile_sems.at[i, chunk]
        )

    list_copies = [
        pltpu.make_async_copy(source, target, list_sems.at[i])
        for i, (source, target) in enumerate(zip(list_hbm, (rows_ref, cols_ref, counts_ref)))
    ]
    parts = [lax.bitwise_xor(blk, jnp.int32(off)) for off, _ in sources]
    for copy in list_copies:
        copy.start()
    for i in range(n_src):
        for k in range(groups):
            start_unit_copy(i, k)
        tile_copy(i, 0).start()
    acc_copy = None
    if not first:
        acc_copy = pltpu.make_async_copy(
            acc_in, base if halves else acc.at[pl.ds(0, nodes)], acc_sem
        )
        if not halves:
            acc_copy.start()
    if first or halves:
        acc[pl.ds(0, nodes), :] = jnp.zeros((nodes, acc.shape[1]), jnp.float32)
    for copy in list_copies:
        copy.wait()
    live = [counts_ref[0, 0, part] for part in parts]
    for i in range(n_src):
        for chunk in range(1, chunks):

            @pl.when(chunk * CHUNK < live[i])
            def _():
                tile_copy(i, chunk).start()

    if acc_copy is not None:
        if halves:
            acc_copy.start()
        else:
            acc_copy.wait()

    def add_tiles(i, base_slot, count):
        for u in range(count):
            slot = base_slot + u
            row = jnp.where(slot < live[i], rows_ref[0, 0, parts[i], slot], row_tiles)
            col = cols_ref[0, 0, parts[i], slot]
            term = lax.dot_general(
                tiles[i, slot],
                feat[i, :, pl.ds(pl.multiple_of(col * size, size), size)],
                (((1,), (1,)), ((), ())),
                preferred_element_type=jnp.float32,
            )
            acc[pl.ds(pl.multiple_of(row * size, size), size), :] += term

    for i in range(n_src):
        for k in range(groups):
            unit_copy(i, k).wait()
        tile_copy(i, 0).wait()
        add_tiles(i, 0, CHUNK)
    for i in range(n_src):
        left = jnp.maximum(live[i] - CHUNK, 0)
        wide = left // WIDE
        narrow = (left - wide * WIDE + CHUNK - 1) // CHUNK

        def do_wide(step, _):
            for part in range(WIDE // CHUNK):
                tile_copy(i, 1 + step * (WIDE // CHUNK) + part).wait()
            add_tiles(i, CHUNK + step * WIDE, WIDE)
            return 0

        def do_narrow(step, _):
            chunk = 1 + wide * (WIDE // CHUNK) + step
            tile_copy(i, chunk).wait()
            add_tiles(i, chunk * CHUNK, CHUNK)
            return 0

        lax.fori_loop(0, wide, do_wide, 0)
        lax.fori_loop(0, narrow, do_narrow, 0)
    if not halves:
        out_copy = pltpu.make_async_copy(acc.at[pl.ds(0, nodes)], out_refs[0], acc_sem)
        out_copy.start()
        out_copy.wait()
        return
    acc_copy.wait()
    share = nodes // groups
    half = share // 2
    for part, bit in ((0, 2), (1, 1)):
        send_ref, keep_ref = out_refs[2 * part : 2 * part + 2]
        for j, step in enumerate((0, 3 ^ bit)):
            mine = lax.bitwise_xor(z, jnp.int32(step)) * share + part * half
            theirs = lax.bitwise_xor(z, jnp.int32(step ^ bit)) * share + part * half
            mine = pl.ds(pl.multiple_of(mine, half), half)
            theirs = pl.ds(pl.multiple_of(theirs, half), half)
            keep_ref[j] = acc[mine, :] + base[mine, :]
            send_ref[j] = (acc[theirs, :] + base[theirs, :]).astype(jnp.bfloat16)


def aggregate(sources, lists, units, acc, halves, earlier=(), hidden=False):
    rows, cols, counts, tiles = lists
    n_src = len(sources)
    groups = len(sources[0][1])
    slots, size = tiles.shape[3], tiles.shape[4]
    width, nodes = units[0].shape[-2:]
    feat_width = width * groups
    any_spec = pl.BlockSpec(memory_space=pl.ANY)
    vmem = pl.BlockSpec(memory_space=pltpu.VMEM)
    if halves:
        dims = (2, nodes // groups // 2, feat_width)
        out_shape = [jax.ShapeDtypeStruct(dims, jnp.bfloat16), jax.ShapeDtypeStruct(dims, jnp.float32)] * 2
        out_spec = vmem
    else:
        out_shape = [jax.ShapeDtypeStruct((nodes, feat_width), jnp.float32)]
        out_spec = any_spec
    extra = [] if acc is None else [acc]
    return pl.pallas_call(
        functools.partial(aggregate_kernel, sources, len(units), len(earlier), halves, acc is None),
        out_shape=tuple(out_shape),
        in_specs=[any_spec] * (4 + len(units) + len(earlier) + len(extra)),
        out_specs=(out_spec,) * len(out_shape),
        scratch_shapes=[
            pltpu.SMEM(rows.shape, jnp.int32),
            pltpu.SMEM(cols.shape, jnp.int32),
            pltpu.SMEM(counts.shape, jnp.int32),
            pltpu.VMEM((n_src, feat_width, nodes), jnp.bfloat16),
            pltpu.VMEM((n_src, slots, size, size), jnp.bfloat16),
            pltpu.VMEM((nodes + size, feat_width), jnp.float32),
            pltpu.VMEM((nodes if halves else 8, feat_width), jnp.float32),
            pltpu.SemaphoreType.DMA((n_src, groups)),
            pltpu.SemaphoreType.DMA((n_src, slots // CHUNK)),
            pltpu.SemaphoreType.DMA((3,)),
            pltpu.SemaphoreType.DMA,
        ],
        compiler_params=pltpu.CompilerParams(vmem_limit_bytes=(8 + 3 * n_src) * 1024 * 1024),
        cost_estimate=pl.CostEstimate(
            flops=0 if hidden else 2 * n_src * slots * size * size * feat_width * 4,
            bytes_accessed=1024 if hidden else n_src * (slots * size * size + feat_width * nodes) * 2,
            transcendentals=0,
        ),
    )(*in_hbm(rows, cols, counts, tiles), *units, *earlier, *extra)


def low_bit(m):
    return m & -m


def plain(first, groups):
    return tuple(((first + k, None),) * 2 for k in range(groups))


def gather_any(features, lists):
    groups, chips = lax.axis_size("feat"), lax.axis_size("blk") // 2
    held = {(0, 0): features}
    for k in range(1, groups):
        bit = low_bit(k)
        held[k, 0] = hop(held[k ^ bit, 0], "feat", bit)
    for k in range(groups):
        for m in range(1, chips):
            bit = low_bit(m) if k % 2 == 0 else 1 << (m.bit_length() - 1)
            held[k, m] = hop(held[k, m ^ bit], "blk", 2 * bit)
    other = {key: hop(value, "blk", 1) for key, value in held.items()}
    acc = None
    for m in range(chips):
        sources, units = [], []
        for side, table in ((0, held), (1, other)):
            sources.append((2 * m + side, plain(len(units), groups)))
            units += [table[k, m] for k in range(groups)]
        acc = aggregate(tuple(sources), lists, units, acc, False)[0]
    return acc


def sum_any(total, groups):
    z = lax.axis_index("feat")
    total = total.reshape(groups, total.shape[0] // groups, total.shape[1])
    bit = 1
    while bit < groups:
        mine = lax.rem(z // bit, 2)
        pairs = total.reshape(total.shape[0] // 2, 2, *total.shape[1:])
        send = lax.dynamic_index_in_dim(pairs, 1 - mine, 1, False).astype(jnp.bfloat16)
        keep = lax.dynamic_index_in_dim(pairs, mine, 1, False)
        total = keep + hop(send, "feat", bit).astype(jnp.float32)
        bit *= 2
    return total[0].astype(jnp.bfloat16)


def gather_2x2x4(features, lists):
    def swap(value):
        return hop(value, "blk", 1)

    def cross(value, even_bit, odd_bit):
        perm = [(i, i ^ (odd_bit if i % 2 else even_bit)) for i in range(8)]
        return lax.ppermute(value, "blk", perm)

    def along_feat(value, even_bit, odd_bit):
        perm = [(i, i ^ (odd_bit if i // 4 % 2 else even_bit)) for i in range(32)]
        return lax.ppermute(value, ("blk", "feat"), perm)

    own, sibling, near, near_too, distant, distant_too = {0: features}, {}, {}, {}, {}, {}
    own[2] = hop(features, "feat", 2)
    own[1] = hop(features, "feat", 1)
    beside = [hop(features, "blk", 2), hop(features, "blk", 4)]
    sibling[0] = swap(features)
    distant[0] = after(cross(pick(beside[1], beside[0]), 2, 4), flops=10**9)
    distant_too[0] = swap(distant[0])
    sibling[1] = swap(own[1])
    near[1] = after(cross(pair_of(own[1], sibling[1]), 2, 4), flops=10**9)
    own[3] = after(hop(own[2], "feat", 1), flops=3*10**9)
    sibling[2] = swap(own[2])
    near[2] = cross(pair_of(own[2], sibling[2]), 2, 4)
    odd_far = after(along_feat(pair_of(distant[0], distant_too[0]), 3, 1), flops=2000000000)
    sibling[3] = swap(own[3])
    near[3] = cross(pair_of(own[3], sibling[3], near[1]), 2, 4)
    units = [own[k] for k in range(4)] + [sibling[k] for k in range(4)]
    sources = ((0, plain(0, 4)), (1, plain(4, 4)))
    acc = aggregate(sources, lists, units, None, False)[0]

    distant[2] = after(cross(pick_part(near[2], acc), 4, 2), flops=8000000000)

    beside_too = [swap(pick(beside[0], beside[0], acc)), swap(beside[1])]
    odd_far_too = swap(odd_far)
    near_too = {k: swap(near[k]) for k in range(1, 4)}
    distant_too[2] = swap(distant[2])
    units = [distant[0], distant[2], distant_too[0], distant_too[2], odd_far, odd_far_too]
    units += [near[k] for k in range(1, 4)] + [near_too[k] for k in range(1, 4)] + beside + beside_too
    sources = []
    for side in range(2):
        alone = [((2 * side + j, None),) * 2 for j in range(2)]
        third = ((4, side), (5, 1 - side))
        first = ((5, side), (4, 1 - side))
        sources.append((6 + side, (alone[0], first, alone[1], third)))
    for along, bit in enumerate((2, 4)):
        for side in range(2):
            slices = [((12 + 2 * side + along, None),) * 2]
            for k in range(1, 4):
                table = (6, 9) if along == 0 else (9, 6)
                slices.append(((table[0] + k - 1, side), (table[1] + k - 1, 1 - side)))
            sources.append((bit + side, tuple(slices)))
    return aggregate(tuple(sources), lists, units, acc, True)


def sum_2x2x4(send_a, keep_a, send_b, keep_b):
    got_a = hop(send_a, "feat", 2).astype(jnp.float32)
    got_b = hop(send_b, "feat", 1).astype(jnp.float32)
    more_a = hop((keep_a[1] + got_a[1]).astype(jnp.bfloat16), "feat", 1).astype(jnp.float32)
    more_b = hop((keep_b[1] + got_b[1]).astype(jnp.bfloat16), "feat", 2).astype(jnp.float32)
    total = [keep_a[0] + got_a[0] + more_a, keep_b[0] + got_b[0] + more_b]
    return jnp.concatenate(total).astype(jnp.bfloat16)


def shards(features, adj_tiles, tile_rows, tile_cols, counts, weight, cotangent):
    blocks = lax.axis_size("blk")
    groups = lax.axis_size("feat")
    width, nodes = features.shape
    feat_width = width * groups
    chips = blocks // 2
    lists = (tile_rows, tile_cols, counts, adj_tiles)

    if blocks == 8 and groups == 4:
        aggregated = sum_2x2x4(*gather_2x2x4(features, lists))
    else:
        aggregated = sum_any(gather_any(features, lists), groups)

    preact = lax.dot_general(
        weight, aggregated, (((1,), (1,)), ((), ())), preferred_element_type=jnp.float32
    )
    sigmoid_z = jax.nn.sigmoid(preact)
    activated = (preact * sigmoid_z).astype(jnp.bfloat16)
    slope = (cotangent.astype(jnp.float32) * sigmoid_z * (1.0 + preact * (1.0 - sigmoid_z))).astype(
        jnp.bfloat16
    )
    local_grad = jnp.dot(slope, aggregated, preferred_element_type=jnp.float32)
    local_grad = local_grad.astype(jnp.bfloat16)
    share = feat_width // groups
    z = lax.axis_index("feat")

    def rows_for(bit):
        return lax.dynamic_slice_in_dim(local_grad, lax.bitwise_xor(z, jnp.int32(bit)) * share, share, 0)

    terms = [hop(rows_for(bit), "feat", bit).astype(jnp.float32) for bit in range(groups - 1, 0, -1)]
    grad = functools.reduce(jnp.add, terms, rows_for(0).astype(jnp.float32))
    sent = grad.astype(jnp.bfloat16)
    grad = sent.astype(jnp.float32) + hop(sent, "blk", 1).astype(jnp.float32)
    sent = grad.astype(jnp.bfloat16)
    parts = [(hop(sent, "blk", 2 * m) if m else sent).astype(jnp.float32) for m in range(chips)]
    while len(parts) > 1:
        parts = [parts[i] + parts[i + 1] for i in range(0, len(parts), 2)]
    return activated, parts[0] * (1.0 / math.sqrt(blocks * nodes))


def solution(mesh):
    in_specs = (
        P("feat", "blk"),
        P("blk", "feat", None, None, None, None),
        P("blk", "feat", None, None),
        P("blk", "feat", None, None),
        P("blk", "feat", None),
        P(),
        P(None, ("blk", "feat")),
    )
    out_specs = (P(None, ("blk", "feat")), P("feat", None))
    return jax.shard_map(shards, mesh=mesh, in_specs=in_specs, out_specs=out_specs, check_vma=False)
```

```python
import functools
import math

import jax
import jax.numpy as jnp
from jax import lax
from jax.experimental import pallas as pl
from jax.experimental.pallas import tpu as pltpu
from jax.sharding import PartitionSpec as P

CHUNK = 8
WIDE = 16


def hop(value, axis, bit):
    size = lax.axis_size(axis)
    return lax.ppermute(value, axis, [(i, i ^ bit) for i in range(size)])


def in_hbm(*values):
    return [pltpu.with_memory_space_constraint(value, pltpu.HBM) for value in values]


def in_vmem(*values):
    return [pltpu.with_memory_space_constraint(value, pltpu.VMEM) for value in values]


def pair_kernel(own_ref, sibling_ref, *refs):
    core = lax.rem(lax.axis_index("blk"), 2)
    refs[-1][core] = own_ref[...]
    refs[-1][1 - core] = sibling_ref[...]


def pick_kernel(even_ref, odd_ref, *refs):
    core = lax.rem(lax.axis_index("blk"), 2)

    @pl.when(core == 0)
    def _():
        refs[-1][...] = even_ref[...]

    @pl.when(core == 1)
    def _():
        refs[-1][...] = odd_ref[...]


def pick_part_kernel(pair_ref, *refs):
    refs[-1][...] = pair_ref[lax.rem(lax.axis_index("blk"), 2)]


def copying(kernel, shape, values, earlier, flops=0):
    vmem = pl.BlockSpec(memory_space=pltpu.VMEM)
    return pl.pallas_call(
        kernel,
        out_shape=pltpu.VMEM(shape, values[0].dtype),
        in_specs=[vmem] * len(values) + [pl.BlockSpec(memory_space=pl.ANY)] * len(earlier),
        out_specs=vmem,
        compiler_params=pltpu.CompilerParams(vmem_limit_bytes=1024 * 1024),
        cost_estimate=pl.CostEstimate(
            flops=flops, bytes_accessed=1024, transcendentals=0
        ),
    )(*in_vmem(*values), *earlier)


def same_kernel(value_ref, *refs):
    refs[-1][...] = value_ref[...]


def after(value, *earlier, flops=0):
    return copying(same_kernel, value.shape, [value], earlier, flops)


def pair_of(own, sibling, *earlier):
    return copying(pair_kernel, (2, *own.shape), [own, sibling], earlier)


def pick(even, odd, *earlier):
    return copying(pick_kernel, even.shape, [even, odd], earlier)


def pick_part(pair, *earlier):
    return copying(pick_part_kernel, pair.shape[1:], [pair], earlier)


def aggregate_kernel(sources, n_units, n_earlier, halves, first, *refs):
    *list_hbm, tiles_ref = refs[:4]
    unit_refs = refs[4 : 4 + n_units]
    rest = list(refs[4 + n_units + n_earlier :])
    acc_in = None if first else rest.pop(0)
    n_out = 4 if halves else 1
    out_refs = rest[:n_out]
    rows_ref, cols_ref, counts_ref, feat, tiles, acc, base, unit_sems, tile_sems, list_sems, acc_sem = rest[
        n_out:
    ]
    blk = lax.axis_index("blk")
    z = lax.axis_index("feat")
    n_src = len(sources)
    groups = len(sources[0][1])
    slots = tiles_ref.shape[3]
    size = tiles_ref.shape[4]
    width, nodes = unit_refs[0].shape[-2:]
    row_tiles = nodes // size
    chunks = slots // CHUNK
    odd = lax.rem(blk, 2) == 1

    def unit_copy(i, k, side=0):
        unit, part = sources[i][1][k][side]
        ref = unit_refs[unit] if part is None else unit_refs[unit].at[part]
        start = pl.multiple_of(lax.bitwise_xor(z, jnp.int32(k)) * width, width)
        return pltpu.make_async_copy(ref, feat.at[i, pl.ds(start, width), :], unit_sems.at[i, k])

    def start_unit_copy(i, k):
        even, on_odd = sources[i][1][k]
        if even == on_odd:
            unit_copy(i, k).start()
            return
        pl.when(jnp.logical_not(odd))(lambda: unit_copy(i, k, 0).start())
        pl.when(odd)(lambda: unit_copy(i, k, 1).start())

    def tile_copy(i, chunk):
        at = pl.ds(chunk * CHUNK, CHUNK)
        return pltpu.make_async_copy(
            tiles_ref.at[0, 0, parts[i], at], tiles.at[i, at], tile_sems.at[i, chunk]
        )

    list_copies = [
        pltpu.make_async_copy(source, target, list_sems.at[i])
        for i, (source, target) in enumerate(zip(list_hbm, (rows_ref, cols_ref, counts_ref)))
    ]
    parts = [lax.bitwise_xor(blk, jnp.int32(off)) for off, _ in sources]
    for copy in list_copies:
        copy.start()
    for i in range(n_src):
        for k in range(groups):
            start_unit_copy(i, k)
        tile_copy(i, 0).start()
    acc_copy = None
    if not first:
        acc_copy = pltpu.make_async_copy(
            acc_in, base if halves else acc.at[pl.ds(0, nodes)], acc_sem
        )
        if not halves:
            acc_copy.start()
    if first or halves:
        acc[pl.ds(0, nodes), :] = jnp.zeros((nodes, acc.shape[1]), jnp.float32)
    for copy in list_copies:
        copy.wait()
    live = [counts_ref[0, 0, part] for part in parts]
    for i in range(n_src):
        for chunk in range(1, chunks):

            @pl.when(chunk * CHUNK < live[i])
            def _():
                tile_copy(i, chunk).start()

    if acc_copy is not None:
        if halves:
            acc_copy.start()
        else:
            acc_copy.wait()

    def add_tiles(i, base_slot, count):
        for u in range(count):
            slot = base_slot + u
            row = jnp.where(slot < live[i], rows_ref[0, 0, parts[i], slot], row_tiles)
            col = cols_ref[0, 0, parts[i], slot]
            term = lax.dot_general(
                tiles[i, slot],
                feat[i, :, pl.ds(pl.multiple_of(col * size, size), size)],
                (((1,), (1,)), ((), ())),
                preferred_element_type=jnp.float32,
            )
            acc[pl.ds(pl.multiple_of(row * size, size), size), :] += term

    for i in range(n_src):
        for k in range(groups):
            unit_copy(i, k).wait()
        tile_copy(i, 0).wait()
        add_tiles(i, 0, CHUNK)
    for i in range(n_src):
        left = jnp.maximum(live[i] - CHUNK, 0)
        wide = left // WIDE
        narrow = (left - wide * WIDE + CHUNK - 1) // CHUNK

        def do_wide(step, _):
            for part in range(WIDE // CHUNK):
                tile_copy(i, 1 + step * (WIDE // CHUNK) + part).wait()
            add_tiles(i, CHUNK + step * WIDE, WIDE)
            return 0

        def do_narrow(step, _):
            chunk = 1 + wide * (WIDE // CHUNK) + step
            tile_copy(i, chunk).wait()
            add_tiles(i, chunk * CHUNK, CHUNK)
            return 0

        lax.fori_loop(0, wide, do_wide, 0)
        lax.fori_loop(0, narrow, do_narrow, 0)
    if not halves:
        out_copy = pltpu.make_async_copy(acc.at[pl.ds(0, nodes)], out_refs[0], acc_sem)
        out_copy.start()
        out_copy.wait()
        return
    acc_copy.wait()
    share = nodes // groups
    half = share // 2
    for part, bit in ((0, 2), (1, 1)):
        send_ref, keep_ref = out_refs[2 * part : 2 * part + 2]
        for j, step in enumerate((0, 3 ^ bit)):
            mine = lax.bitwise_xor(z, jnp.int32(step)) * share + part * half
            theirs = lax.bitwise_xor(z, jnp.int32(step ^ bit)) * share + part * half
            mine = pl.ds(pl.multiple_of(mine, half), half)
            theirs = pl.ds(pl.multiple_of(theirs, half), half)
            keep_ref[j] = acc[mine, :] + base[mine, :]
            send_ref[j] = (acc[theirs, :] + base[theirs, :]).astype(jnp.bfloat16)


def aggregate(sources, lists, units, acc, halves, earlier=(), hidden=False):
    rows, cols, counts, tiles = lists
    n_src = len(sources)
    groups = len(sources[0][1])
    slots, size = tiles.shape[3], tiles.shape[4]
    width, nodes = units[0].shape[-2:]
    feat_width = width * groups
    any_spec = pl.BlockSpec(memory_space=pl.ANY)
    vmem = pl.BlockSpec(memory_space=pltpu.VMEM)
    if halves:
        dims = (2, nodes // groups // 2, feat_width)
        out_shape = [jax.ShapeDtypeStruct(dims, jnp.bfloat16), jax.ShapeDtypeStruct(dims, jnp.float32)] * 2
        out_spec = vmem
    else:
        out_shape = [jax.ShapeDtypeStruct((nodes, feat_width), jnp.float32)]
        out_spec = any_spec
    extra = [] if acc is None else [acc]
    return pl.pallas_call(
        functools.partial(aggregate_kernel, sources, len(units), len(earlier), halves, acc is None),
        out_shape=tuple(out_shape),
        in_specs=[any_spec] * (4 + len(units) + len(earlier) + len(extra)),
        out_specs=(out_spec,) * len(out_shape),
        scratch_shapes=[
            pltpu.SMEM(rows.shape, jnp.int32),
            pltpu.SMEM(cols.shape, jnp.int32),
            pltpu.SMEM(counts.shape, jnp.int32),
            pltpu.VMEM((n_src, feat_width, nodes), jnp.bfloat16),
            pltpu.VMEM((n_src, slots, size, size), jnp.bfloat16),
            pltpu.VMEM((nodes + size, feat_width), jnp.float32),
            pltpu.VMEM((nodes if halves else 8, feat_width), jnp.float32),
            pltpu.SemaphoreType.DMA((n_src, groups)),
            pltpu.SemaphoreType.DMA((n_src, slots // CHUNK)),
            pltpu.SemaphoreType.DMA((3,)),
            pltpu.SemaphoreType.DMA,
        ],
        compiler_params=pltpu.CompilerParams(vmem_limit_bytes=(8 + 3 * n_src) * 1024 * 1024),
        cost_estimate=pl.CostEstimate(
            flops=0 if hidden else 2 * n_src * slots * size * size * feat_width * 4,
            bytes_accessed=1024 if hidden else n_src * (slots * size * size + feat_width * nodes) * 2,
            transcendentals=0,
        ),
    )(*in_hbm(rows, cols, counts, tiles), *units, *earlier, *extra)


def low_bit(m):
    return m & -m


def plain(first, groups):
    return tuple(((first + k, None),) * 2 for k in range(groups))


def gather_any(features, lists):
    groups, chips = lax.axis_size("feat"), lax.axis_size("blk") // 2
    held = {(0, 0): features}
    for k in range(1, groups):
        bit = low_bit(k)
        held[k, 0] = hop(held[k ^ bit, 0], "feat", bit)
    for k in range(groups):
        for m in range(1, chips):
            bit = low_bit(m) if k % 2 == 0 else 1 << (m.bit_length() - 1)
            held[k, m] = hop(held[k, m ^ bit], "blk", 2 * bit)
    other = {key: hop(value, "blk", 1) for key, value in held.items()}
    acc = None
    for m in range(chips):
        sources, units = [], []
        for side, table in ((0, held), (1, other)):
            sources.append((2 * m + side, plain(len(units), groups)))
            units += [table[k, m] for k in range(groups)]
        acc = aggregate(tuple(sources), lists, units, acc, False)[0]
    return acc


def sum_any(total, groups):
    z = lax.axis_index("feat")
    total = total.reshape(groups, total.shape[0] // groups, total.shape[1])
    bit = 1
    while bit < groups:
        mine = lax.rem(z // bit, 2)
        pairs = total.reshape(total.shape[0] // 2, 2, *total.shape[1:])
        send = lax.dynamic_index_in_dim(pairs, 1 - mine, 1, False).astype(jnp.bfloat16)
        keep = lax.dynamic_index_in_dim(pairs, mine, 1, False)
        total = keep + hop(send, "feat", bit).astype(jnp.float32)
        bit *= 2
    return total[0].astype(jnp.bfloat16)


def gather_2x2x4(features, lists):
    def swap(value):
        return hop(value, "blk", 1)

    def cross(value, even_bit, odd_bit):
        perm = [(i, i ^ (odd_bit if i % 2 else even_bit)) for i in range(8)]
        return lax.ppermute(value, "blk", perm)

    def along_feat(value, even_bit, odd_bit):
        perm = [(i, i ^ (odd_bit if i // 4 % 2 else even_bit)) for i in range(32)]
        return lax.ppermute(value, ("blk", "feat"), perm)

    own, sibling, near, near_too, distant, distant_too = {0: features}, {}, {}, {}, {}, {}
    own[2] = hop(features, "feat", 2)
    own[1] = hop(features, "feat", 1)
    beside = [hop(features, "blk", 2), hop(features, "blk", 4)]
    sibling[0] = swap(features)
    distant[0] = after(cross(pick(beside[1], beside[0]), 2, 4), flops=10**9)
    distant_too[0] = swap(distant[0])
    sibling[1] = swap(own[1])
    near[1] = after(cross(pair_of(own[1], sibling[1]), 2, 4), flops=10**9)
    own[3] = after(hop(own[2], "feat", 1), flops=3*10**9)
    sibling[2] = swap(own[2])
    near[2] = cross(pair_of(own[2], sibling[2]), 2, 4)
    odd_far = after(along_feat(pair_of(distant[0], distant_too[0]), 3, 1), flops=2000000000)
    sibling[3] = swap(own[3])
    near[3] = cross(pair_of(own[3], sibling[3], near[1]), 2, 4)
    units = [own[k] for k in range(4)] + [sibling[k] for k in range(4)]
    sources = ((0, plain(0, 4)), (1, plain(4, 4)))
    acc = aggregate(sources, lists, units, None, False)[0]

    distant[2] = after(cross(pick_part(near[2], acc), 4, 2), flops=8000000000)

    beside_too = [swap(pick(beside[0], beside[0], acc)), swap(beside[1])]
    odd_far_too = swap(odd_far)
    near_too = {k: swap(near[k]) for k in range(1, 4)}
    distant_too[2] = swap(distant[2])
    units = [distant[0], distant[2], distant_too[0], distant_too[2], odd_far, odd_far_too]
    units += [near[k] for k in range(1, 4)] + [near_too[k] for k in range(1, 4)] + beside + beside_too
    sources = []
    for side in range(2):
        alone = [((2 * side + j, None),) * 2 for j in range(2)]
        third = ((4, side), (5, 1 - side))
        first = ((5, side), (4, 1 - side))
        sources.append((6 + side, (alone[0], first, alone[1], third)))
    for along, bit in enumerate((2, 4)):
        for side in range(2):
            slices = [((12 + 2 * side + along, None),) * 2]
            for k in range(1, 4):
                table = (6, 9) if along == 0 else (9, 6)
                slices.append(((table[0] + k - 1, side), (table[1] + k - 1, 1 - side)))
            sources.append((bit + side, tuple(slices)))
    return aggregate(tuple(sources), lists, units, acc, True)


def sum_2x2x4(send_a, keep_a, send_b, keep_b):
    got_a = hop(send_a, "feat", 2).astype(jnp.float32)
    got_b = hop(send_b, "feat", 1).astype(jnp.float32)
    more_a = hop((keep_a[1] + got_a[1]).astype(jnp.bfloat16), "feat", 1).astype(jnp.float32)
    more_b = hop((keep_b[1] + got_b[1]).astype(jnp.bfloat16), "feat", 2).astype(jnp.float32)
    total = [keep_a[0] + got_a[0] + more_a, keep_b[0] + got_b[0] + more_b]
    return jnp.concatenate(total).astype(jnp.bfloat16)


def shards(features, adj_tiles, tile_rows, tile_cols, counts, weight, cotangent):
    blocks = lax.axis_size("blk")
    groups = lax.axis_size("feat")
    width, nodes = features.shape
    feat_width = width * groups
    chips = blocks // 2
    lists = (tile_rows, tile_cols, counts, adj_tiles)

    if blocks == 8 and groups == 4:
        aggregated = sum_2x2x4(*gather_2x2x4(features, lists))
    else:
        aggregated = sum_any(gather_any(features, lists), groups)

    preact = lax.dot_general(
        weight, aggregated, (((1,), (1,)), ((), ())), preferred_element_type=jnp.float32
    )
    sigmoid_z = jax.nn.sigmoid(preact)
    activated = (preact * sigmoid_z).astype(jnp.bfloat16)
    slope = (cotangent.astype(jnp.float32) * sigmoid_z * (1.0 + preact * (1.0 - sigmoid_z))).astype(
        jnp.bfloat16
    )
    local_grad = jnp.dot(slope, aggregated, preferred_element_type=jnp.float32)
    local_grad = local_grad.astype(jnp.bfloat16)
    share = feat_width // groups
    z = lax.axis_index("feat")

    def rows_for(bit):
        return lax.dynamic_slice_in_dim(local_grad, lax.bitwise_xor(z, jnp.int32(bit)) * share, share, 0)

    terms = [hop(rows_for(bit), "feat", bit).astype(jnp.float32) for bit in range(groups - 1, 0, -1)]
    grad = functools.reduce(jnp.add, terms, rows_for(0).astype(jnp.float32))
    sent = grad.astype(jnp.bfloat16)
    grad = sent.astype(jnp.float32) + hop(sent, "blk", 1).astype(jnp.float32)
    sent = grad.astype(jnp.bfloat16)
    got = {m: hop(sent, "blk", 2 * m) for m in range(chips - 1, 0, -1)}
    parts = [(got[m] if m else sent).astype(jnp.float32) for m in range(chips)]
    while len(parts) > 1:
        parts = [parts[i] + parts[i + 1] for i in range(0, len(parts), 2)]
    return activated, parts[0] * (1.0 / math.sqrt(blocks * nodes))


def solution(mesh):
    in_specs = (
        P("feat", "blk"),
        P("blk", "feat", None, None, None, None),
        P("blk", "feat", None, None),
        P("blk", "feat", None, None),
        P("blk", "feat", None),
        P(),
        P(None, ("blk", "feat")),
    )
    out_specs = (P(None, ("blk", "feat")), P("feat", None))
    return jax.shard_map(shards, mesh=mesh, in_specs=in_specs, out_specs=out_specs, check_vma=False)
```
